32 devices in a mesh: section: 4 (over z), seq: 8 (over y, x, core).
Axes of the slice: x: 2, y: 2, z: 4, core: 2. Of those that a mesh axis runs over, the one named last changes fastest.
Arguments:
- tokens: bfloat16 [4, 64, 8192], P('section', 'seq'), may hold values from -6 to 6
- norm_gain: bfloat16 [4, 8192], P('section'), may hold values from 0.099609375 to 1.8984375
- w_query: bfloat16 [4, 8192, 8192], P('section', None, 'seq'), may hold values from -0.0625 to 0.0625
- key_projection: bfloat16 [4, 8192, 1024], P('section', None, 'seq'), may hold values from -0.1875 to 0.1875
- value_projection: bfloat16 [4, 8192, 1024], P('section', None, 'seq'), may hold values from -0.0625 to 0.0625
- w_out: bfloat16 [4, 8192, 8192], P('section', 'seq'), may hold values from -0.0625 to 0.0625
- key_cache: bfloat16 [4, 16384, 8, 128], P('section', 'seq'), may hold values from -400 to 400
- cached_value_rows: bfloat16 [4, 16384, 8, 128], P('section', 'seq'), may hold values from -6 to 6
- cache_mask: int32 [4, 2, 128], P('section', None, 'seq'), may hold values 0 or 1
- span_offset: int32 [4], P('section'), may hold values from 0 to 32767
Outputs:
- handed: bfloat16 [4, 64, 8192], P('section', 'seq')
The draws below stay inside these ranges and needn't reach their ends.
All inputs are finite; a program needn't handle non-finite values. No bound on the sum of `cache_mask` on one device may be relied on, other than what follows from the above.
Results may differ from the reference program's by a relative error of at most 0.014.
Values may be sent and summed in bfloat16 or wider, within the bound.
No kernel may reach another device: no remote copies, remote signals or barrier semaphores. Data moves between devices by JAX's collectives and lax.ppermute only.
A program may use at most 192 MiB of HBM per device.

```python
import jax
import jax.numpy as jnp
from jax import lax

MODEL_WIDTH = 8192
HQ = 64
KEY_VALUE_HEADS = 8
HEAD_SIZE = 128
GROUP = 8
QB = 32
KB = 128
RELAY_SECTIONS = 4
SECTION_TOKENS = 64
CONTEXT_LENGTH = 16384
NQB = 2
NKB = 128


def draw_key_cache(key, part):
    first = jax.random.fold_in(key, 0)
    array_shape = (RELAY_SECTIONS, CONTEXT_LENGTH, KEY_VALUE_HEADS, HEAD_SIZE)
    values = 2.2 * jnp.clip(jax.random.normal(first, array_shape, jnp.float32), -6.0, 6.0)
    return values.astype(jnp.bfloat16)


def plant(entries, own_key, smallest, high):
    shape = entries.shape
    index_at = [jax.random.randint(jax.random.fold_in(own_key, axis), (), 0, shape[axis]) for axis in range(len(shape))]
    entries = entries.at[tuple(index_at)].set(smallest)
    longest = shape.index(max(shape))
    index_at[longest] = (index_at[longest] + 1) % shape[longest]
    return entries.at[tuple(index_at)].set(high)


def level_of(rng, shape, cuts, low, high):
    level, own = 1.0, jax.random.fold_in(rng, 6)
    for axis_at, blocks in cuts:
        steps = jnp.exp(jax.random.uniform(jax.random.fold_in(own, axis_at), (blocks,), jnp.float32, low / len(cuts), high / len(cuts)))
        level = level * jnp.repeat(steps, shape[axis_at] // blocks).reshape([-1 if axis == axis_at else 1 for axis in range(len(shape))])
    return level


def gaussian(stream_key, dims, width, reach, cuts=(), kind=jnp.bfloat16):
    level = level_of(stream_key, dims, cuts, -0.22, 0.18) if cuts else 1.0
    entries = jax.random.normal(stream_key, dims, jnp.float32) * width * level
    return jnp.minimum(jnp.maximum(entries, -reach), reach).astype(kind)


def setup_inputs(seed: int = 0) -> dict:
    streams_of = jax.random.split(jax.random.key(seed), 11)
    return {
        "tokens": gaussian(streams_of[0], (RELAY_SECTIONS, SECTION_TOKENS, MODEL_WIDTH), 1.0, 6.0, ((0, 4), (1, 8))),
        "norm_gain": jnp.clip(1.0 + 0.18 * jax.random.normal(streams_of[1], (RELAY_SECTIONS, MODEL_WIDTH), jnp.float32), 0.099609375, 1.8984375).astype(jnp.bfloat16),
        "w_query": gaussian(streams_of[2], (RELAY_SECTIONS, MODEL_WIDTH, HQ * HEAD_SIZE), MODEL_WIDTH ** -0.5, 0.0625, ((0, 4), (2, 8))),
        "key_projection": gaussian(streams_of[3], (RELAY_SECTIONS, MODEL_WIDTH, KEY_VALUE_HEADS * HEAD_SIZE), (MODEL_WIDTH // 9) ** -0.5, 0.1875, ((0, 4), (2, 8))),
        "value_projection": gaussian(streams_of[4], (RELAY_SECTIONS, MODEL_WIDTH, KEY_VALUE_HEADS * HEAD_SIZE), MODEL_WIDTH ** -0.5, 0.0625, ((0, 4), (2, 8))),
        "w_out": gaussian(streams_of[5], (RELAY_SECTIONS, HQ * HEAD_SIZE, MODEL_WIDTH), (HQ * HEAD_SIZE) ** -0.5, 0.0625, ((0, 4), (1, 8))),
        "key_cache": draw_key_cache(jax.random.fold_in(streams_of[10], 71), 0),
        "cached_value_rows": gaussian(streams_of[7], (RELAY_SECTIONS, CONTEXT_LENGTH, KEY_VALUE_HEADS, HEAD_SIZE), 1.0, 6.0, ((0, 4), (1, 8))),
        "cache_mask": plant((jax.random.randint(streams_of[8], (RELAY_SECTIONS, NQB, NKB), 0, 4) < 1).astype(jnp.int32), jax.random.fold_in(streams_of[8], 1), 0, 1),
        "span_offset": plant(jax.random.randint(streams_of[9], (RELAY_SECTIONS,), 0, 32768), jax.random.fold_in(streams_of[9], 1), 0, 32767).astype(jnp.int32),
    }


rope_base = 500000.0
neg_fill = -1e+30
norm_eps = 1e-05

def apply_rotation(values, token_positions):
    half = values.shape[-1] // 2
    freqs = rope_base ** (-2.0 * jnp.arange(half, dtype=jnp.float32) / values.shape[-1])
    angles = token_positions[:, None] * freqs[None, :]
    cosine = jnp.cos(angles)[:, None, :]
    sine = jnp.sin(angles)[:, None, :]
    first = values[..., :half]
    second = values[..., half:]
    return jnp.concatenate([first * cosine - second * sine, second * cosine + first * sine], axis=-1)

def one_layer(tokens, gain, w_query, key_projection, value_projection, w_out, key_cache, cached_value_rows, mask, offset):
    resid = tokens.astype(jnp.float32)
    mean_square = lax.optimization_barrier(jnp.mean(resid * resid, axis=-1, keepdims=True))
    input_normalized = (resid * lax.rsqrt(mean_square + norm_eps) * gain.astype(jnp.float32)).astype(jnp.bfloat16)
    token_positions = offset.astype(jnp.float32) + jnp.arange(SECTION_TOKENS, dtype=jnp.int32).astype(jnp.float32)
    query = jnp.dot(input_normalized, w_query, preferred_element_type=jnp.float32).reshape(SECTION_TOKENS, HQ, HEAD_SIZE)
    query = apply_rotation(query, token_positions).astype(jnp.bfloat16)
    key_unrotated = jnp.dot(input_normalized, key_projection, preferred_element_type=jnp.float32).astype(jnp.bfloat16)
    value_rows = jnp.dot(input_normalized, value_projection, preferred_element_type=jnp.float32).astype(jnp.bfloat16).reshape(SECTION_TOKENS, KEY_VALUE_HEADS, HEAD_SIZE)
    key = apply_rotation(key_unrotated.astype(jnp.float32).reshape(SECTION_TOKENS, KEY_VALUE_HEADS, HEAD_SIZE), token_positions).astype(jnp.bfloat16)
    visible = jnp.broadcast_to(mask[:, None, :, None] > 0, (NQB, QB, NKB, KB)).reshape(SECTION_TOKENS, CONTEXT_LENGTH)
    rows = jnp.arange(SECTION_TOKENS, dtype=jnp.int32)
    causal = rows[None, :] <= rows[:, None]
    scale = HEAD_SIZE ** (-0.5)

    def head_fn(item):
        query_head, head_id = item
        group_index = head_id // GROUP
        cache_keys = lax.dynamic_index_in_dim(key_cache, group_index, 1, keepdims=False)
        cache_values = lax.dynamic_index_in_dim(cached_value_rows, group_index, 1, keepdims=False)
        new_keys = lax.dynamic_index_in_dim(key, group_index, 1, keepdims=False)
        new_values = lax.dynamic_index_in_dim(value_rows, group_index, 1, keepdims=False)
        cache_scores = jnp.dot(query_head, cache_keys.T, preferred_element_type=jnp.float32) * scale
        self_scores = jnp.dot(query_head, new_keys.T, preferred_element_type=jnp.float32) * scale
        cache_scores = jnp.where(visible, cache_scores, neg_fill)
        self_scores = jnp.where(causal, self_scores, neg_fill)
        top = jnp.maximum(lax.optimization_barrier(jnp.max(cache_scores, axis=1)), lax.optimization_barrier(jnp.max(self_scores, axis=1)))
        cache_weights = jnp.where(visible, jnp.exp(cache_scores - top[:, None]), 0.0)
        self_weights = jnp.where(causal, jnp.exp(self_scores - top[:, None]), 0.0)
        total = lax.optimization_barrier(jnp.sum(cache_weights, axis=1)) + lax.optimization_barrier(jnp.sum(self_weights, axis=1))
        summed = jnp.dot(cache_weights.astype(jnp.bfloat16), cache_values, preferred_element_type=jnp.float32)
        summed = summed + jnp.dot(self_weights.astype(jnp.bfloat16), new_values, preferred_element_type=jnp.float32)
        return (summed / total[:, None]).astype(jnp.bfloat16)
    heads_out = lax.map(head_fn, (jnp.transpose(query, (1, 0, 2)), jnp.arange(HQ, dtype=jnp.int32)))
    attention = jnp.transpose(heads_out, (1, 0, 2)).reshape(SECTION_TOKENS, HQ * HEAD_SIZE)
    projected = jnp.dot(attention, w_out, preferred_element_type=jnp.float32)
    return (resid + projected).astype(jnp.bfloat16)

def reference(tokens, norm_gain, w_query, key_projection, value_projection, w_out, key_cache, cached_value_rows, cache_mask, span_offset):
    results = []
    for section_index in range(RELAY_SECTIONS):
        results.append(one_layer(tokens[section_index], norm_gain[section_index], w_query[section_index], key_projection[section_index], value_projection[section_index], w_out[section_index], key_cache[section_index], cached_value_rows[section_index], cache_mask[section_index], span_offset[section_index]))
    stacked = jnp.stack(results, axis=0)
    return jnp.roll(stacked, 1, axis=0)
```

```python
import jax
import jax.numpy as jnp
from jax import lax
from jax.experimental import pallas as pl
from jax.experimental.pallas import tpu as pltpu
from jax.sharding import PartitionSpec as P

QB = 32
KB = 128


rope_base = 500000.0
neg_fill = -1e30
norm_eps = 1e-05


def passed_along(block, axis, distance):
    devices = range(lax.axis_size(axis))
    route = [((i - distance) % len(devices), i) for i in devices]
    return lax.ppermute(block, axis, route)


def apply_rotation(values, token_positions):
    half = values.shape[-1] // 2
    freqs = rope_base ** (-2.0 * jnp.arange(half, dtype=jnp.float32) / values.shape[-1])
    angles = token_positions[:, None] * freqs[None, :]
    cosine = jnp.cos(angles)[:, None, :]
    sine = jnp.sin(angles)[:, None, :]
    first = values[..., :half]
    second = values[..., half:]
    return jnp.concatenate(
        [first * cosine - second * sine, second * cosine + first * sine], axis=-1
    )


def on_device_any(
    tokens,
    norm_gain,
    w_query,
    key_projection,
    value_projection,
    w_out,
    key_cache,
    cached_value_rows,
    cache_mask,
    span_offset,
):
    n_seq = lax.axis_size("seq")
    rank = lax.axis_index("seq")
    head_dim = key_cache.shape[3]
    kv_heads = key_cache.shape[2]
    own_heads = w_query.shape[2] // head_dim
    all_heads = own_heads * n_seq
    group = all_heads // kv_heads
    tok_local = tokens.shape[1]
    tok_all = tok_local * n_seq
    ctx_local = key_cache.shape[1]
    scale = head_dim ** (-0.5)
    query_cols = own_heads * head_dim
    key_cols = key_projection.shape[2]
    offset = span_offset[0].astype(jnp.float32)
    resid = tokens[0].astype(jnp.float32)
    mean_square = jnp.mean(resid * resid, axis=-1, keepdims=True)
    input_normalized = (
        resid * lax.rsqrt(mean_square + norm_eps) * norm_gain[0].astype(jnp.float32)
    ).astype(jnp.bfloat16)
    piece = lax.all_gather(input_normalized, "seq", axis=0, tiled=True)
    rows = piece.shape[0]
    token_positions = offset + jnp.arange(rows, dtype=jnp.int32).astype(jnp.float32)
    query = jnp.dot(piece, w_query[0], preferred_element_type=jnp.float32)
    query = apply_rotation(query.reshape(rows, own_heads, head_dim), token_positions).reshape(
        rows, query_cols
    )
    key_unrotated = jnp.dot(piece, key_projection[0], preferred_element_type=jnp.float32)
    value_raw = jnp.dot(piece, value_projection[0], preferred_element_type=jnp.float32)
    fresh = jnp.concatenate([query, key_unrotated, value_raw], axis=1).astype(jnp.bfloat16)
    own_query = fresh[:, :query_cols]
    query_all, key_all, value_all = (
        lax.all_gather(own_query, "seq", axis=1, tiled=True),
        lax.all_gather(fresh[:, query_cols : query_cols + key_cols], "seq", axis=1, tiled=True),
        lax.all_gather(fresh[:, query_cols + key_cols :], "seq", axis=1, tiled=True),
    )
    positions_all = offset + jnp.arange(tok_all, dtype=jnp.int32).astype(jnp.float32)
    key_rot = apply_rotation(
        key_all.astype(jnp.float32).reshape(tok_all, kv_heads, head_dim), positions_all
    ).astype(jnp.bfloat16)
    value_heads = value_all.reshape(tok_all, kv_heads, head_dim)
    query_grouped = query_all.reshape(tok_all, kv_heads, group, head_dim)
    block = min(512, ctx_local)
    per_block = block // KB
    q_blocks = tok_all // QB

    def cache_step(index, carry):
        top, total, summed = carry
        keys = lax.dynamic_slice_in_dim(key_cache[0], index * block, block, 0)
        values = lax.dynamic_slice_in_dim(cached_value_rows[0], index * block, block, 0)
        visible = lax.dynamic_slice_in_dim(cache_mask[0], index * per_block, per_block, 1) > 0
        scores = (
            jnp.einsum("tgjd,cgd->tgjc", query_grouped, keys, preferred_element_type=jnp.float32)
            * scale
        )
        shaped = scores.reshape(q_blocks, QB, kv_heads, group, per_block, KB)
        allowed = visible[:, None, None, None, :, None]
        shaped = jnp.where(allowed, shaped, neg_fill)
        block_top = jnp.max(shaped, axis=(4, 5)).reshape(tok_all, kv_heads, group)
        new_top = jnp.maximum(top, block_top)
        lifted = new_top.reshape(q_blocks, QB, kv_heads, group, 1, 1)
        weights = jnp.where(allowed, jnp.exp(shaped - lifted), 0.0).reshape(
            tok_all, kv_heads, group, block
        )
        factor = jnp.exp(top - new_top)
        total = total * factor + jnp.sum(weights, axis=-1)
        summed = summed * factor[..., None] + jnp.einsum(
            "tgjc,cgd->tgjd",
            weights.astype(jnp.bfloat16),
            values,
            preferred_element_type=jnp.float32,
        )
        return (new_top, total, summed)

    start_top = jnp.full((tok_all, kv_heads, group), neg_fill, jnp.float32)
    start_total = jnp.zeros((tok_all, kv_heads, group), jnp.float32)
    start_sum = jnp.zeros((tok_all, kv_heads, group, head_dim), jnp.float32)
    top, total, summed = lax.fori_loop(
        0, ctx_local // block, cache_step, (start_top, start_total, start_sum)
    )
    top = top.reshape(tok_all, all_heads)
    total = total.reshape(tok_all, all_heads)
    summed = summed.reshape(tok_all, all_heads, head_dim)
    got_sum, got_top, got_total = (
        lax.all_to_all(summed[None], "seq", split_axis=2, concat_axis=0, tiled=True),
        lax.all_to_all(top[None], "seq", split_axis=2, concat_axis=0, tiled=True),
        lax.all_to_all(total[None], "seq", split_axis=2, concat_axis=0, tiled=True),
    )
    cache_top = jnp.max(got_top, axis=0)
    factor = jnp.exp(got_top - cache_top[None])
    cache_total = jnp.sum(got_total * factor, axis=0)
    cache_sum = jnp.sum(got_sum * factor[..., None], axis=0)
    kv_index = (rank * own_heads + jnp.arange(own_heads, dtype=jnp.int32)) // group
    own_keys = jnp.take(key_rot, kv_index, axis=1)
    own_values = jnp.take(value_heads, kv_index, axis=1)
    own_q = own_query.reshape(tok_all, own_heads, head_dim)
    self_scores = (
        jnp.einsum("thd,shd->ths", own_q, own_keys, preferred_element_type=jnp.float32) * scale
    )
    row_ids = jnp.arange(tok_all, dtype=jnp.int32)
    causal = (row_ids[None, :] <= row_ids[:, None])[:, None, :]
    self_scores = jnp.where(causal, self_scores, neg_fill)
    top_all = jnp.maximum(cache_top, jnp.max(self_scores, axis=-1))
    cache_factor = jnp.exp(cache_top - top_all)
    self_weights = jnp.where(causal, jnp.exp(self_scores - top_all[..., None]), 0.0)
    total_all = cache_total * cache_factor + jnp.sum(self_weights, axis=-1)
    sum_all = cache_sum * cache_factor[..., None] + jnp.einsum(
        "ths,shd->thd",
        self_weights.astype(jnp.bfloat16),
        own_values,
        preferred_element_type=jnp.float32,
    )
    attention = (sum_all / total_all[..., None]).reshape(tok_all, query_cols).astype(jnp.bfloat16)
    projected = lax.psum_scatter(
        jnp.dot(attention, w_out[0], preferred_element_type=jnp.float32).astype(jnp.bfloat16),
        "seq",
        scatter_dimension=0,
        tiled=True,
    ).astype(jnp.float32)
    layer_out = (resid + projected).astype(jnp.bfloat16)
    handed = passed_along(layer_out, "section", 1)
    return handed[None]


MIB = 1 << 20
log2e = 1.4426950408889634
IN_VMEM = pl.BlockSpec(memory_space=pltpu.VMEM)
IN_SMEM = pl.BlockSpec(memory_space=pltpu.SMEM)
SAME_CORE = (2, 4, 6)
EVEN = (0, 2, 4, 6)
ODD = (1, 3, 5, 7)


def swapped(block, bits):
    n = lax.axis_size("seq")
    return lax.ppermute(block, "seq", [(i, i ^ bits) for i in range(n)])


def call(kernel, name, out_shape, in_specs, flops=0, nbytes=0, scratch=(), vmem=16, **grid):
    out_specs = grid.pop("out_specs", jax.tree.map(lambda _: IN_VMEM, out_shape))
    return pl.pallas_call(
        kernel,
        out_shape=out_shape,
        in_specs=in_specs,
        out_specs=out_specs,
        scratch_shapes=list(scratch),
        name=name,
        cost_estimate=pl.CostEstimate(flops=flops, bytes_accessed=nbytes, transcendentals=0),
        compiler_params=pltpu.CompilerParams(vmem_limit_bytes=vmem * MIB),
        **grid,
    )


def held(array):
    return pltpu.with_memory_space_constraint(array, pltpu.VMEM)


def by_head_kernel(keys, values, keys_out, values_out):
    keys_out[...] = jnp.swapaxes(keys[...], 0, 1)
    turned = jnp.swapaxes(values[...], 0, 1)
    for g in range(turned.shape[0]):
        values_out[g] = turned[g].T


def cache_by_head(keys, values):
    ctx, heads, dim = keys.shape
    block = 256
    source = pl.BlockSpec((block, heads, dim), lambda i: (i, 0, 0))
    return call(
        by_head_kernel,
        "cache_by_head",
        [
            jax.ShapeDtypeStruct((heads, ctx, dim), jnp.bfloat16),
            jax.ShapeDtypeStruct((heads, dim, ctx), jnp.bfloat16),
        ],
        [source, source],
        nbytes=4 * ctx * heads * dim * 2,
        grid=(ctx // block,),
        out_specs=[
            pl.BlockSpec((heads, block, dim), lambda i: (0, i, 0)),
            pl.BlockSpec((heads, dim, block), lambda i: (0, 0, i)),
        ],
    )(keys, values)


def rotated(heads, cosine, sine):
    half = heads.shape[1] // 2
    return heads * cosine + pltpu.roll(heads, half, 1) * sine


def query_kernel(rank, *refs):
    blocks = refs[:8]
    gain, cosine, sine, weights, query, normed, rows = refs[8:]
    width = rows.shape[1]
    count = blocks[0].shape[0]
    step = 1024
    for bits in range(8):
        at = pl.multiple_of((rank[0] ^ bits) * count, count)
        rows[pl.ds(at, count), :] = blocks[bits][...].astype(jnp.float32)
    squares = jnp.zeros((rows.shape[0], 128), jnp.float32)
    for c in range(0, width, 128):
        part = rows[:, c : c + 128]
        squares = squares + part * part
    mean_square = jnp.sum(squares, axis=-1, keepdims=True) / width
    factor = lax.rsqrt(mean_square + norm_eps)
    for c in range(0, width, step):
        normed[:, c : c + step] = (
            rows[:, c : c + step] * factor * gain[:, c : c + step].astype(jnp.float32)
        ).astype(jnp.bfloat16)
    dim = cosine.shape[1]
    for c in range(0, weights.shape[1], 2 * dim):
        raw = jnp.dot(
            normed[...], weights[:, c : c + 2 * dim], preferred_element_type=jnp.float32
        )
        for d in range(0, 2 * dim, dim):
            query[:, c + d : c + d + dim] = rotated(
                raw[:, d : d + dim], cosine[...], sine[...]
            ).astype(jnp.bfloat16)


def query_rows(query, q_block, heads, dim):
    rows = slice(q_block * QB, (q_block + 1) * QB)
    return jnp.concatenate([query[rows, j * dim : (j + 1) * dim] for j in range(heads)], axis=0)


def matmul_nt(a, b):
    return lax.dot_general(a, b, (((1,), (1,)), ((), ())), preferred_element_type=jnp.float32)


def new_kernel(scale, query, normed, w_key, w_value, cosine, sine, summed, stats):
    tok, dim = cosine.shape
    heads = query.shape[1] // dim
    raw = jnp.dot(normed[...], w_key[...], preferred_element_type=jnp.float32)
    raw = raw.astype(jnp.bfloat16).astype(jnp.float32)
    keys = rotated(raw, cosine[...], sine[...]).astype(jnp.bfloat16)
    values = jnp.dot(normed[...], w_value[...], preferred_element_type=jnp.float32)
    values = values.astype(jnp.bfloat16).astype(jnp.float32).T.astype(jnp.bfloat16)
    cols = heads * QB
    for q_block in range(tok // QB):
        scores = matmul_nt(keys, query_rows(query, q_block, heads, dim)) * scale
        u = lax.broadcasted_iota(jnp.int32, (tok, cols), 0)
        t = lax.broadcasted_iota(jnp.int32, (tok, cols), 1) % QB + q_block * QB
        allowed = u <= t
        scores = jnp.where(allowed, scores, neg_fill)
        top = jnp.max(scores, axis=0, keepdims=True)
        weights = jnp.where(allowed, jnp.exp2(scores - top), 0.0)
        at = slice(q_block * cols, (q_block + 1) * cols)
        stats[0:1, at] = top
        stats[1:2, at] = jnp.sum(weights, axis=0, keepdims=True)
        summed[:, at] = jnp.dot(
            values, weights.astype(jnp.bfloat16), preferred_element_type=jnp.float32
        )


def split_rows(level, rows):
    high = level.astype(jnp.bfloat16).astype(jnp.float32)
    rest = level - high
    middle = rest.astype(jnp.bfloat16).astype(jnp.float32)
    low = rest - middle
    row = lax.broadcasted_iota(jnp.int32, (rows, level.shape[1]), 0)
    return jnp.where(row == 0, high, jnp.where(row == 1, middle, jnp.where(row == 2, low, 0.0)))


def level_of(tail):
    tail = tail.astype(jnp.float32)
    return tail[0:1] + tail[1:2] + tail[2:3]


def cache_kernel(scale, order, rank, mask, *refs):
    queries = refs[:4]
    keys, values, out, q_rows, summed, visible = refs[4:]
    dim = keys.shape[2]
    heads = queries[0].shape[1] // dim
    cols = heads * QB
    tail = out.shape[1] - dim
    groups = [rank[0] ^ bits for bits in order]
    for q_block in range(mask.shape[0]):
        count = jnp.int32(0)
        for b in range(mask.shape[1]):
            visible[count] = b
            count = count + (mask[q_block, b] > 0).astype(jnp.int32)
        visible[count] = 0
        for i in range(4):
            q_rows[i] = query_rows(queries[i], q_block, heads, dim)
            summed[i] = jnp.zeros((dim, cols), jnp.float32)

        def step(pair, carry):
            at_first = pl.multiple_of(visible[2 * pair] * KB, KB)
            at_second = pl.multiple_of(visible[2 * pair + 1] * KB, KB)
            hidden = jnp.where(2 * pair + 1 < count, jnp.float32(0.0), jnp.float32(neg_fill))
            after = []
            for i in range(4):
                top, total = carry[2 * i], carry[2 * i + 1]
                g = groups[i]
                first = matmul_nt(keys[g, pl.ds(at_first, KB), :], q_rows[i]) * scale
                second = matmul_nt(keys[g, pl.ds(at_second, KB), :], q_rows[i]) * scale + hidden
                new_top = jnp.maximum(
                    top,
                    jnp.maximum(
                        jnp.max(first, axis=0, keepdims=True),
                        jnp.max(second, axis=0, keepdims=True),
                    ),
                )
                first = jnp.exp2(first - new_top)
                second = jnp.exp2(second - new_top)
                factor = jnp.exp2(top - new_top)
                total = (
                    total * factor
                    + jnp.sum(first, axis=0, keepdims=True)
                    + jnp.sum(second, axis=0, keepdims=True)
                )
                weights = jnp.concatenate([first, second], axis=0).astype(jnp.bfloat16)
                block = jnp.concatenate(
                    [values[g, :, pl.ds(at_first, KB)], values[g, :, pl.ds(at_second, KB)]], axis=1
                )
                summed[i] = summed[i] * factor + jnp.dot(
                    block, weights, preferred_element_type=jnp.float32
                )
                after += [new_top, total]
            return tuple(after)

        start = (jnp.full((1, cols), neg_fill, jnp.float32), jnp.zeros((1, cols), jnp.float32)) * 4
        ended = lax.fori_loop(0, (count + 1) // 2, step, start)
        at = slice(q_block * cols, (q_block + 1) * cols)
        for i in range(4):
            top, total = ended[2 * i], ended[2 * i + 1]
            seen = total > 0.0
            safe = jnp.where(seen, total, 1.0)
            level = jnp.where(seen, top + jnp.log2(safe), neg_fill)
            out[i, 0:dim, at] = (summed[i] / safe).astype(out.dtype)
            out[i, dim:, at] = split_rows(level, tail).astype(out.dtype)


def cache_part(scale, order, rank, mask, queries, keys, values, dtype, name):
    heads, ctx, dim = keys.shape
    cols = (queries[0].shape[1] // dim) * QB
    tail = 16 if dtype == jnp.bfloat16 else 8
    return call(
        lambda *refs: cache_kernel(scale, order, *refs),
        name,
        jax.ShapeDtypeStruct((4, dim + tail, mask.shape[0] * cols), dtype),
        [IN_SMEM, IN_SMEM] + [IN_VMEM] * 6,
        flops=4 * 4 * queries[0].shape[0] * heads * ctx * dim // 4,
        nbytes=4 * MIB,
        scratch=[
            pltpu.VMEM((4, cols, dim), jnp.bfloat16),
            pltpu.VMEM((4, dim, cols), jnp.float32),
            pltpu.SMEM((mask.shape[1] + 2,), jnp.int32),
        ],
    )(rank, mask, *queries, held(keys), held(values))


def merge_kernel(own, got, kept, *sent):
    dim = own.shape[1] - 8
    for i in range(4):
        mine, other = level_of(own[i, dim:, :]), level_of(got[i, dim:, :])
        top = jnp.maximum(mine, other)
        mine, other = jnp.exp2(mine - top), jnp.exp2(other - top)
        total = mine + other
        level = top + jnp.log2(total)
        mine, other = mine / total, other / total
        joined = own[i, :dim, :] * mine + got[i, :dim, :].astype(jnp.float32) * other
        target = kept if i == 0 else sent[i - 1]
        target[:dim, :] = joined.astype(target.dtype)
        target[dim:, :] = split_rows(level, target.shape[0] - dim).astype(target.dtype)


def output_kernel(rank, kept, got_a, got_b, got_c, summed, stats, weights, own, sent, rows, sorted_rows):
    dim = summed.shape[0]
    levels = [level_of(part[dim:, :]) for part in (kept, got_a, got_b, got_c)]
    top = stats[0:1, :]
    for level in levels:
        top = jnp.maximum(top, level)
    factor = jnp.exp2(stats[0:1, :] - top)
    total = stats[1:2, :] * factor
    joined = summed[...] * factor
    for part, level in zip((kept, got_a, got_b, got_c), levels):
        factor = jnp.exp2(level - top)
        total = total + factor
        joined = joined + part[:dim, :].astype(jnp.float32) * factor
    joined = joined / total
    heads = rows.shape[1] // dim
    cols = heads * QB
    for q_block in range(rows.shape[0] // QB):
        turned = joined[:, q_block * cols : (q_block + 1) * cols].T
        for j in range(heads):
            rows[q_block * QB : (q_block + 1) * QB, j * dim : (j + 1) * dim] = turned[
                j * QB : (j + 1) * QB, :
            ]
    count = rows.shape[0] // 8
    for pair in range(4):
        chunk = [
            rows[pl.ds(pl.multiple_of((rank[0] ^ bits) * count, count), count), :]
            for bits in (EVEN + ODD)[2 * pair : 2 * pair + 2]
        ]
        sorted_rows[2 * count * pair : 2 * count * (pair + 1), :] = jnp.concatenate(
            chunk, axis=0
        ).astype(jnp.bfloat16)
    half = rows.shape[0] // 2
    step = 512
    for c in range(0, weights.shape[1], step):
        product = jnp.dot(
            sorted_rows[...], weights[:, c : c + step], preferred_element_type=jnp.float32
        )
        own[:, c : c + step] = product[:half]
        sent[:, c : c + step] = product[half:].astype(jnp.bfloat16)


def on_device_owned(
    tokens,
    norm_gain,
    w_query,
    key_projection,
    value_projection,
    w_out,
    key_cache,
    cached_value_rows,
    cache_mask,
    span_offset,
):
    n_seq = lax.axis_size("seq")
    rank = lax.axis_index("seq").astype(jnp.int32)[None]
    dim = key_cache.shape[3]
    count = tokens.shape[1]
    width = tokens.shape[2]
    tok = count * n_seq
    own_cols = w_query.shape[2]
    scale = dim ** (-0.5) * log2e
    mask = cache_mask[0]

    with jax.named_scope("gather_tokens"):
        blocks = {0: tokens[0]}
        blocks[1] = swapped(tokens[0], 1)
        for bits in SAME_CORE:
            blocks[bits] = swapped(tokens[0], bits)
        for bits in SAME_CORE:
            blocks[bits ^ 1] = swapped(blocks[bits], 1)

    with jax.named_scope("tables"):
        positions = span_offset[0].astype(jnp.float32) + jnp.arange(tok, dtype=jnp.int32).astype(
            jnp.float32
        )
        freqs = rope_base ** (-2.0 * jnp.arange(dim // 2, dtype=jnp.float32) / dim)
        angles = positions[:, None] * freqs[None, :]
        cosine, sine = jnp.cos(angles), jnp.sin(angles)
        cosine = jnp.concatenate([cosine, cosine], axis=1)
        sine = jnp.concatenate([-sine, sine], axis=1)

    with jax.named_scope("cache_layout"):
        keys, values = cache_by_head(key_cache[0], cached_value_rows[0])

    with jax.named_scope("queries"):
        query, normed = call(
            query_kernel,
            "queries",
            [
                jax.ShapeDtypeStruct((tok, own_cols), jnp.bfloat16),
                jax.ShapeDtypeStruct((tok, width), jnp.bfloat16),
            ],
            [IN_SMEM] + [IN_VMEM] * 12,
            flops=2 * tok * width * own_cols,
            nbytes=16 * MIB,
            scratch=[pltpu.VMEM((tok, width), jnp.float32)],
        )(
            rank,
            *[blocks[bits] for bits in range(8)],
            norm_gain,
            cosine,
            sine,
            held(w_query[0]),
        )

    with jax.named_scope("gather_queries"):
        queries = {0: query}
        for bits in ODD:
            queries[bits] = swapped(query, bits)
        for bits in SAME_CORE:
            queries[bits] = swapped(queries[bits ^ 1], 1)

    with jax.named_scope("new_tokens"):
        summed, stats = call(
            lambda *refs: new_kernel(scale, *refs),
            "new_tokens",
            [
                jax.ShapeDtypeStruct((dim, tok * own_cols // dim), jnp.float32),
                jax.ShapeDtypeStruct((8, tok * own_cols // dim), jnp.float32),
            ],
            [IN_VMEM] * 6,
            flops=4 * tok * width * dim,
            nbytes=5 * MIB,
        )(query, normed, held(key_projection[0]), held(value_projection[0]), cosine, sine)

    with jax.named_scope("cache_odd"):
        odd = cache_part(
            scale, ODD, rank, mask, [queries[b] for b in ODD], keys, values, jnp.bfloat16, "cache_odd"
        )
    with jax.named_scope("swap_odd"):
        got = swapped(odd, 1)
    with jax.named_scope("cache_even"):
        even = cache_part(
            scale, EVEN, rank, mask, [queries[b] for b in EVEN], keys, values, jnp.float32, "cache_even"
        )
    with jax.named_scope("merge_cores"):
        cols = even.shape[2]
        kept, *sent = call(
            merge_kernel,
            "merge_cores",
            [jax.ShapeDtypeStruct((dim + 8, cols), jnp.float32)]
            + [jax.ShapeDtypeStruct((dim + 16, cols), jnp.bfloat16)] * 3,
            [IN_VMEM] * 2,
            nbytes=2 * MIB,
        )(even, got)
    with jax.named_scope("exchange_parts"):
        parts = [swapped(block, bits) for block, bits in zip(sent, SAME_CORE)]
    with jax.named_scope("project"):
        own, other = call(
            output_kernel,
            "project",
            [
                jax.ShapeDtypeStruct((tok // 2, width), jnp.float32),
                jax.ShapeDtypeStruct((tok // 2, width), jnp.bfloat16),
            ],
            [IN_SMEM] + [IN_VMEM] * 7,
            flops=2 * tok * width * own_cols,
            nbytes=18 * MIB,
            scratch=[
                pltpu.VMEM((tok, own_cols), jnp.float32),
                pltpu.VMEM((tok, own_cols), jnp.bfloat16),
            ],
        )(rank, kept, *parts, summed, stats, held(w_out[0]))
    with jax.named_scope("reduce_cores"):
        pair = own + swapped(other, 1).astype(jnp.float32)
    with jax.named_scope("reduce_chips"):
        total = tokens[0].astype(jnp.float32) + pair[:count]
        for i, bits in enumerate(SAME_CORE):
            block = pair[(i + 1) * count : (i + 2) * count].astype(jnp.bfloat16)
            total = total + swapped(block, bits).astype(jnp.float32)
        layer_out = total.astype(jnp.bfloat16)
    with jax.named_scope("hand_on"):
        handed = passed_along(layer_out, "section", 1)
    return handed[None]


def on_device(*arrays):
    tokens, w_query, key_projection, key_cache = arrays[0], arrays[2], arrays[3], arrays[6]
    head_dim = key_cache.shape[3]
    kv_heads = key_cache.shape[2]
    n_seq = lax.axis_size("seq")
    tok_all = tokens.shape[1] * n_seq
    if (
        n_seq == kv_heads == 8
        and key_projection.shape[2] == head_dim == 128
        and tokens.shape[1] == 8
        and tok_all == 2 * QB
    ):
        return on_device_owned(*arrays)
    return on_device_any(*arrays)


def solution(mesh):
    placed = (
        P("section", "seq", None),
        P("section", None),
        P("section", None, "seq"),
        P("section", None, "seq"),
        P("section", None, "seq"),
        P("section", "seq", None),
        P("section", "seq", None, None),
        P("section", "seq", None, None),
        P("section", None, "seq"),
        P("section"),
    )
    return jax.shard_map(
        on_device, mesh=mesh, in_specs=placed, out_specs=P("section", "seq", None), check_vma=False
    )
```

```python
import jax
import jax.numpy as jnp
from jax import lax
from jax.experimental import pallas as pl
from jax.experimental.pallas import tpu as pltpu
from jax.sharding import PartitionSpec as P

QB = 32
KB = 128


rope_base = 500000.0
neg_fill = -1e30
norm_eps = 1e-05


def passed_along(block, axis, distance):
    devices = range(lax.axis_size(axis))
    route = [((i - distance) % len(devices), i) for i in devices]
    return lax.ppermute(block, axis, route)


def apply_rotation(values, token_positions):
    half = values.shape[-1] // 2
    freqs = rope_base ** (-2.0 * jnp.arange(half, dtype=jnp.float32) / values.shape[-1])
    angles = token_positions[:, None] * freqs[None, :]
    cosine = jnp.cos(angles)[:, None, :]
    sine = jnp.sin(angles)[:, None, :]
    first = values[..., :half]
    second = values[..., half:]
    return jnp.concatenate(
        [first * cosine - second * sine, second * cosine + first * sine], axis=-1
    )


def on_device_any(
    tokens,
    norm_gain,
    w_query,
    key_projection,
    value_projection,
    w_out,
    key_cache,
    cached_value_rows,
    cache_mask,
    span_offset,
):
    n_seq = lax.axis_size("seq")
    rank = lax.axis_index("seq")
    head_dim = key_cache.shape[3]
    kv_heads = key_cache.shape[2]
    own_heads = w_query.shape[2] // head_dim
    all_heads = own_heads * n_seq
    group = all_heads // kv_heads
    tok_local = tokens.shape[1]
    tok_all = tok_local * n_seq
    ctx_local = key_cache.shape[1]
    scale = head_dim ** (-0.5)
    query_cols = own_heads * head_dim
    key_cols = key_projection.shape[2]
    offset = span_offset[0].astype(jnp.float32)
    resid = tokens[0].astype(jnp.float32)
    mean_square = jnp.mean(resid * resid, axis=-1, keepdims=True)
    input_normalized = (
        resid * lax.rsqrt(mean_square + norm_eps) * norm_gain[0].astype(jnp.float32)
    ).astype(jnp.bfloat16)
    piece = lax.all_gather(input_normalized, "seq", axis=0, tiled=True)
    rows = piece.shape[0]
    token_positions = offset + jnp.arange(rows, dtype=jnp.int32).astype(jnp.float32)
    query = jnp.dot(piece, w_query[0], preferred_element_type=jnp.float32)
    query = apply_rotation(query.reshape(rows, own_heads, head_dim), token_positions).reshape(
        rows, query_cols
    )
    key_unrotated = jnp.dot(piece, key_projection[0], preferred_element_type=jnp.float32)
    value_raw = jnp.dot(piece, value_projection[0], preferred_element_type=jnp.float32)
    fresh = jnp.concatenate([query, key_unrotated, value_raw], axis=1).astype(jnp.bfloat16)
    own_query = fresh[:, :query_cols]
    query_all, key_all, value_all = (
        lax.all_gather(own_query, "seq", axis=1, tiled=True),
        lax.all_gather(fresh[:, query_cols : query_cols + key_cols], "seq", axis=1, tiled=True),
        lax.all_gather(fresh[:, query_cols + key_cols :], "seq", axis=1, tiled=True),
    )
    positions_all = offset + jnp.arange(tok_all, dtype=jnp.int32).astype(jnp.float32)
    key_rot = apply_rotation(
        key_all.astype(jnp.float32).reshape(tok_all, kv_heads, head_dim), positions_all
    ).astype(jnp.bfloat16)
    value_heads = value_all.reshape(tok_all, kv_heads, head_dim)
    query_grouped = query_all.reshape(tok_all, kv_heads, group, head_dim)
    block = min(512, ctx_local)
    per_block = block // KB
    q_blocks = tok_all // QB

    def cache_step(index, carry):
        top, total, summed = carry
        keys = lax.dynamic_slice_in_dim(key_cache[0], index * block, block, 0)
        values = lax.dynamic_slice_in_dim(cached_value_rows[0], index * block, block, 0)
        visible = lax.dynamic_slice_in_dim(cache_mask[0], index * per_block, per_block, 1) > 0
        scores = (
            jnp.einsum("tgjd,cgd->tgjc", query_grouped, keys, preferred_element_type=jnp.float32)
            * scale
        )
        shaped = scores.reshape(q_blocks, QB, kv_heads, group, per_block, KB)
        allowed = visible[:, None, None, None, :, None]
        shaped = jnp.where(allowed, shaped, neg_fill)
        block_top = jnp.max(shaped, axis=(4, 5)).reshape(tok_all, kv_heads, group)
        new_top = jnp.maximum(top, block_top)
        lifted = new_top.reshape(q_blocks, QB, kv_heads, group, 1, 1)
        weights = jnp.where(allowed, jnp.exp(shaped - lifted), 0.0).reshape(
            tok_all, kv_heads, group, block
        )
        factor = jnp.exp(top - new_top)
        total = total * factor + jnp.sum(weights, axis=-1)
        summed = summed * factor[..., None] + jnp.einsum(
            "tgjc,cgd->tgjd",
            weights.astype(jnp.bfloat16),
            values,
            preferred_element_type=jnp.float32,
        )
        return (new_top, total, summed)

    start_top = jnp.full((tok_all, kv_heads, group), neg_fill, jnp.float32)
    start_total = jnp.zeros((tok_all, kv_heads, group), jnp.float32)
    start_sum = jnp.zeros((tok_all, kv_heads, group, head_dim), jnp.float32)
    top, total, summed = lax.fori_loop(
        0, ctx_local // block, cache_step, (start_top, start_total, start_sum)
    )
    top = top.reshape(tok_all, all_heads)
    total = total.reshape(tok_all, all_heads)
    summed = summed.reshape(tok_all, all_heads, head_dim)
    got_sum, got_top, got_total = (
        lax.all_to_all(summed[None], "seq", split_axis=2, concat_axis=0, tiled=True),
        lax.all_to_all(top[None], "seq", split_axis=2, concat_axis=0, tiled=True),
        lax.all_to_all(total[None], "seq", split_axis=2, concat_axis=0, tiled=True),
    )
    cache_top = jnp.max(got_top, axis=0)
    factor = jnp.exp(got_top - cache_top[None])
    cache_total = jnp.sum(got_total * factor, axis=0)
    cache_sum = jnp.sum(got_sum * factor[..., None], axis=0)
    kv_index = (rank * own_heads + jnp.arange(own_heads, dtype=jnp.int32)) // group
    own_keys = jnp.take(key_rot, kv_index, axis=1)
    own_values = jnp.take(value_heads, kv_index, axis=1)
    own_q = own_query.reshape(tok_all, own_heads, head_dim)
    self_scores = (
        jnp.einsum("thd,shd->ths", own_q, own_keys, preferred_element_type=jnp.float32) * scale
    )
    row_ids = jnp.arange(tok_all, dtype=jnp.int32)
    causal = (row_ids[None, :] <= row_ids[:, None])[:, None, :]
    self_scores = jnp.where(causal, self_scores, neg_fill)
    top_all = jnp.maximum(cache_top, jnp.max(self_scores, axis=-1))
    cache_factor = jnp.exp(cache_top - top_all)
    self_weights = jnp.where(causal, jnp.exp(self_scores - top_all[..., None]), 0.0)
    total_all = cache_total * cache_factor + jnp.sum(self_weights, axis=-1)
    sum_all = cache_sum * cache_factor[..., None] + jnp.einsum(
        "ths,shd->thd",
        self_weights.astype(jnp.bfloat16),
        own_values,
        preferred_element_type=jnp.float32,
    )
    attention = (sum_all / total_all[..., None]).reshape(tok_all, query_cols).astype(jnp.bfloat16)
    projected = lax.psum_scatter(
        jnp.dot(attention, w_out[0], preferred_element_type=jnp.float32).astype(jnp.bfloat16),
        "seq",
        scatter_dimension=0,
        tiled=True,
    ).astype(jnp.float32)
    layer_out = (resid + projected).astype(jnp.bfloat16)
    handed = passed_along(layer_out, "section", 1)
    return handed[None]


MIB = 1 << 20
log2e = 1.4426950408889634
IN_VMEM = pl.BlockSpec(memory_space=pltpu.VMEM)
IN_SMEM = pl.BlockSpec(memory_space=pltpu.SMEM)
SAME_CORE = (2, 4, 6)
EVEN = (0, 2, 4, 6)
ODD = (1, 3, 5, 7)


def swapped(block, bits):
    n = lax.axis_size("seq")
    return lax.ppermute(block, "seq", [(i, i ^ bits) for i in range(n)])


def call(kernel, name, out_shape, in_specs, flops=0, nbytes=0, scratch=(), vmem=6, **grid):
    out_specs = grid.pop("out_specs", jax.tree.map(lambda _: IN_VMEM, out_shape))
    return pl.pallas_call(
        kernel,
        out_shape=out_shape,
        in_specs=in_specs,
        out_specs=out_specs,
        scratch_shapes=list(scratch),
        name=name,
        cost_estimate=pl.CostEstimate(flops=flops, bytes_accessed=nbytes, transcendentals=0),
        compiler_params=pltpu.CompilerParams(vmem_limit_bytes=vmem * MIB),
        **grid,
    )


def held(array):
    return pltpu.with_memory_space_constraint(array, pltpu.VMEM)


def join_kernel(count, *refs):
    for i in range(count):
        refs[-1][i] = refs[i][...]


def joined_after(blocks, done, name):
    count = len(blocks)
    return call(
        lambda *refs: join_kernel(count, *refs),
        name,
        jax.ShapeDtypeStruct((count, *blocks[0].shape), blocks[0].dtype),
        [IN_VMEM] * count + [pl.BlockSpec(memory_space=pl.ANY)] * len(done),
        nbytes=MIB,
        vmem=2,
    )(*blocks, *done)


def rotated(heads, cosine, sine):
    half = heads.shape[1] // 2
    return heads * cosine + pltpu.roll(heads, half, 1) * sine


def query_kernel(rank, *refs):
    mine, near, far, far_near = refs[:4]
    gain, cosine, sine, weights, query, normed, rows = refs[4:]
    width = rows.shape[1]
    count = mine.shape[0]
    blocks = [mine, near] + [part.at[i] for i in range(3) for part in (far, far_near)]
    step = 1024
    for bits in range(8):
        at = pl.multiple_of((rank[0] ^ bits) * count, count)
        rows[pl.ds(at, count), :] = blocks[bits][...].astype(jnp.float32)
    squares = jnp.zeros((rows.shape[0], 128), jnp.float32)
    for c in range(0, width, 128):
        part = rows[:, c : c + 128]
        squares = squares + part * part
    mean_square = jnp.sum(squares, axis=-1, keepdims=True) / width
    factor = lax.rsqrt(mean_square + norm_eps)
    for c in range(0, width, step):
        normed[:, c : c + step] = (
            rows[:, c : c + step] * factor * gain[:, c : c + step].astype(jnp.float32)
        ).astype(jnp.bfloat16)
    dim = cosine.shape[1]
    for c in range(0, weights.shape[1], 2 * dim):
        raw = jnp.dot(
            normed[...], weights[:, c : c + 2 * dim], preferred_element_type=jnp.float32
        )
        for d in range(0, 2 * dim, dim):
            query[:, c + d : c + d + dim] = rotated(
                raw[:, d : d + dim], cosine[...], sine[...]
            ).astype(jnp.bfloat16)


def query_rows(query, q_block, heads, dim):
    rows = slice(q_block * QB, (q_block + 1) * QB)
    return jnp.concatenate([query[rows, j * dim : (j + 1) * dim] for j in range(heads)], axis=0)


def matmul_nt(a, b):
    return lax.dot_general(a, b, (((1,), (1,)), ((), ())), preferred_element_type=jnp.float32)


def keys_kernel(rank, keys, keys_out, done):
    keys_out[...] = jnp.swapaxes(keys[...], 0, 1)
    done[...] = jnp.zeros_like(done)


def keys_by_head(rank, keys):
    ctx, heads, dim = keys.shape
    block = 256
    return call(
        keys_kernel,
        "keys_by_head",
        [
            jax.ShapeDtypeStruct((heads, ctx, dim), jnp.bfloat16),
            jax.ShapeDtypeStruct((8, 128), jnp.float32),
        ],
        [IN_SMEM, pl.BlockSpec((block, heads, dim), lambda i: (i, 0, 0))],
        flops=10**10,
        nbytes=2 * ctx * heads * dim * 2,
        grid=(ctx // block,),
        out_specs=[
            pl.BlockSpec((heads, block, dim), lambda i: (0, i, 0)),
            pl.BlockSpec((8, 128), lambda i: (0, 0)),
        ],
    )(rank, pltpu.with_memory_space_constraint(keys, pltpu.HBM))


def values_by_head(values, values_out):
    block = 256

    @pl.loop(0, values.shape[0] // block)
    def _(i):
        at = pl.ds(pl.multiple_of(i * block, block), block)
        turned = jnp.swapaxes(values[at], 0, 1)
        for g in range(turned.shape[0]):
            values_out[g, :, at] = turned[g].T


def new_kernel(
    scale,
    query,
    normed,
    w_key,
    w_value,
    cosine,
    sine,
    cached_values,
    values_out,
    summed,
    stats,
):
    values_by_head(cached_values, values_out)
    tok, dim = cosine.shape
    heads = query.shape[1] // dim
    raw = jnp.dot(normed[...], w_key[...], preferred_element_type=jnp.float32)
    raw = raw.astype(jnp.bfloat16).astype(jnp.float32)
    keys = rotated(raw, cosine[...], sine[...]).astype(jnp.bfloat16)
    values = jnp.dot(normed[...], w_value[...], preferred_element_type=jnp.float32)
    values = values.astype(jnp.bfloat16).astype(jnp.float32).T.astype(jnp.bfloat16)
    cols = heads * QB
    for q_block in range(tok // QB):
        scores = matmul_nt(keys, query_rows(query, q_block, heads, dim)) * scale
        u = lax.broadcasted_iota(jnp.int32, (tok, cols), 0)
        t = lax.broadcasted_iota(jnp.int32, (tok, cols), 1) % QB + q_block * QB
        allowed = u <= t
        scores = jnp.where(allowed, scores, neg_fill)
        top = jnp.max(scores, axis=0, keepdims=True)
        weights = jnp.where(allowed, jnp.exp2(scores - top), 0.0)
        at = slice(q_block * cols, (q_block + 1) * cols)
        stats[0:1, at] = top
        stats[1:2, at] = jnp.sum(weights, axis=0, keepdims=True)
        summed[:, at] = jnp.dot(
            values, weights.astype(jnp.bfloat16), preferred_element_type=jnp.float32
        )


def split_rows(level, rows):
    high = level.astype(jnp.bfloat16).astype(jnp.float32)
    rest = level - high
    middle = rest.astype(jnp.bfloat16).astype(jnp.float32)
    low = rest - middle
    row = lax.broadcasted_iota(jnp.int32, (rows, level.shape[1]), 0)
    return jnp.where(row == 0, high, jnp.where(row == 1, middle, jnp.where(row == 2, low, 0.0)))


def level_of(tail):
    tail = tail.astype(jnp.float32)
    return tail[0:1] + tail[1:2] + tail[2:3]


def cache_kernel(scale, order, rank, mask, *refs):
    n = len(order)
    given = 1 if len(refs[0].shape) == 3 else n
    queries, (keys, values), outs = refs[:given], refs[given : given + 2], refs[given + 2 : -3]
    if given < n:
        queries = [queries[0].at[i] for i in range(n)]
    q_rows, summed, visible = refs[-3:]
    dim = keys.shape[2]
    heads = queries[0].shape[1] // dim
    cols = heads * QB
    groups = [rank[0] ^ bits for bits in order]
    own = [bits for bits in order if bits in EVEN]
    for q_block in range(mask.shape[0]):
        count = jnp.int32(0)
        for b in range(mask.shape[1]):
            visible[count] = b
            count = count + (mask[q_block, b] > 0).astype(jnp.int32)
        visible[count] = 0
        for i in range(n):
            q_rows[i] = query_rows(queries[i], q_block, heads, dim)
            summed[i] = jnp.zeros((dim, cols), jnp.float32)

        def step(pair, carry):
            at = [pl.multiple_of(visible[2 * pair + e] * KB, KB) for e in range(2)]
            hidden = jnp.where(2 * pair + 1 < count, jnp.float32(0.0), jnp.float32(neg_fill))
            scores = [
                matmul_nt(
                    jnp.concatenate([keys[g, pl.ds(a, KB), :] for a in at], axis=0), q_rows[i]
                )
                for i, g in enumerate(groups)
            ]
            levels, scaled = [], []
            for i in range(n):
                top, total = carry[2 * i], carry[2 * i + 1]
                first = scores[i][:KB] * scale
                second = scores[i][KB:] * scale + hidden
                new_top = jnp.maximum(
                    top, jnp.max(jnp.maximum(first, second), axis=0, keepdims=True)
                )
                first = jnp.exp2(first - new_top)
                second = jnp.exp2(second - new_top)
                factor = jnp.exp2(top - new_top)
                total = total * factor + jnp.sum(first + second, axis=0, keepdims=True)
                levels += [new_top, total]
                weights = jnp.concatenate(
                    [first.astype(jnp.bfloat16), second.astype(jnp.bfloat16)], axis=0
                )
                scaled.append((factor, weights))
            products = [
                jnp.dot(
                    jnp.concatenate([values[g, :, pl.ds(a, KB)] for a in at], axis=1),
                    scaled[i][1],
                    preferred_element_type=jnp.float32,
                )
                for i, g in enumerate(groups)
            ]
            for i in range(n):
                summed[i] = summed[i] * scaled[i][0] + products[i]
            return tuple(levels)

        start = (jnp.full((1, cols), neg_fill, jnp.float32), jnp.zeros((1, cols), jnp.float32)) * n
        ended = lax.fori_loop(0, (count + 1) // 2, step, start)
        at = slice(q_block * cols, (q_block + 1) * cols)
        for i, bits in enumerate(order):
            top, total = ended[2 * i], ended[2 * i + 1]
            seen = total > 0.0
            safe = jnp.where(seen, total, 1.0)
            level = jnp.where(seen, top + jnp.log2(safe), neg_fill)
            if bits in EVEN:
                out, place = outs[0], own.index(bits)
            else:
                out, place = outs[-1], i - len(own)
            out[place, 0:dim, at] = (summed[i] / safe).astype(out.dtype)
            out[place, dim:, at] = split_rows(level, out.shape[1] - dim).astype(out.dtype)


def cache_part(scale, order, rank, mask, queries, keys, values, name):
    heads, ctx, dim = keys.shape
    cols = (queries[0].shape[-1] // dim) * QB
    n = len(order)
    own = len([bits for bits in order if bits in EVEN])
    outs = []
    if own:
        outs.append(jax.ShapeDtypeStruct((own, dim + 8, mask.shape[0] * cols), jnp.float32))
    if n > own:
        outs.append(jax.ShapeDtypeStruct((n - own, dim + 16, mask.shape[0] * cols), jnp.bfloat16))
    return call(
        lambda *refs: cache_kernel(scale, order, *refs),
        name,
        outs,
        [IN_SMEM, IN_SMEM] + [IN_VMEM] * (len(queries) + 2),
        flops=(2 if own else 10) * n * queries[0].shape[-2] * heads * ctx * dim,
        nbytes=n * MIB,
        scratch=[
            pltpu.VMEM((n, cols, dim), jnp.bfloat16),
            pltpu.VMEM((n, dim, cols), jnp.float32),
            pltpu.SMEM((mask.shape[1] + 2,), jnp.int32),
        ],
    )(rank, mask, *queries, held(keys), held(values))


def merge_kernel(own_first, own_rest, got_first, got_rest, kept, *sent):
    dim = own_first.shape[1] - 8
    for i in range(4):
        own = own_first.at[0] if i == 0 else own_rest.at[i - 1]
        got = got_first.at[0] if i == 0 else got_rest.at[i - 1]
        mine, other = level_of(own[dim:, :]), level_of(got[dim:, :])
        top = jnp.maximum(mine, other)
        mine, other = jnp.exp2(mine - top), jnp.exp2(other - top)
        total = mine + other
        level = top + jnp.log2(total)
        mine, other = mine / total, other / total
        joined = own[:dim, :] * mine + got[:dim, :].astype(jnp.float32) * other
        target = kept if i == 0 else sent[i - 1]
        target[:dim, :] = joined.astype(target.dtype)
        target[dim:, :] = split_rows(level, target.shape[0] - dim).astype(target.dtype)


def output_kernel(rank, kept, got_a, got_b, got_c, summed, stats, weights, own, sent, rows, sorted_rows):
    dim = summed.shape[0]
    levels = [level_of(part[dim:, :]) for part in (kept, got_a, got_b, got_c)]
    top = stats[0:1, :]
    for level in levels:
        top = jnp.maximum(top, level)
    factor = jnp.exp2(stats[0:1, :] - top)
    total = stats[1:2, :] * factor
    joined = summed[...] * factor
    for part, level in zip((kept, got_a, got_b, got_c), levels):
        factor = jnp.exp2(level - top)
        total = total + factor
        joined = joined + part[:dim, :].astype(jnp.float32) * factor
    joined = joined / total
    heads = rows.shape[1] // dim
    cols = heads * QB
    for q_block in range(rows.shape[0] // QB):
        turned = joined[:, q_block * cols : (q_block + 1) * cols].T
        for j in range(heads):
            rows[q_block * QB : (q_block + 1) * QB, j * dim : (j + 1) * dim] = turned[
                j * QB : (j + 1) * QB, :
            ]
    count = rows.shape[0] // 8
    for pair in range(4):
        chunk = [
            rows[pl.ds(pl.multiple_of((rank[0] ^ bits) * count, count), count), :]
            for bits in (EVEN + ODD)[2 * pair : 2 * pair + 2]
        ]
        sorted_rows[2 * count * pair : 2 * count * (pair + 1), :] = jnp.concatenate(
            chunk, axis=0
        ).astype(jnp.bfloat16)
    half = rows.shape[0] // 2
    step = 512
    for c in range(0, weights.shape[1], step):
        product = jnp.dot(
            sorted_rows[...], weights[:, c : c + step], preferred_element_type=jnp.float32
        )
        own[:, c : c + step] = product[:half]
        sent[:, c : c + step] = product[half:].astype(jnp.bfloat16)


def on_device_owned(
    tokens,
    norm_gain,
    w_query,
    key_projection,
    value_projection,
    w_out,
    key_cache,
    cached_value_rows,
    cache_mask,
    span_offset,
):
    n_seq = lax.axis_size("seq")
    rank = lax.axis_index("seq").astype(jnp.int32)[None]
    dim = key_cache.shape[3]
    count = tokens.shape[1]
    width = tokens.shape[2]
    tok = count * n_seq
    own_cols = w_query.shape[2]
    scale = dim ** (-0.5) * log2e
    mask = cache_mask[0]

    with jax.named_scope("cache_layout"):
        keys, layout_done = keys_by_head(rank, key_cache[0])
    with jax.named_scope("gather_tokens"):
        blocks = {0: tokens[0]}
        blocks[1] = swapped(tokens[0], 1)
        for bits in SAME_CORE:
            blocks[bits] = swapped(tokens[0], bits)
        far = joined_after([blocks[bits] for bits in SAME_CORE], [layout_done], "join_tokens")
        far_near = swapped(far, 1)

    with jax.named_scope("tables"):
        positions = span_offset[0].astype(jnp.float32) + jnp.arange(tok, dtype=jnp.int32).astype(
            jnp.float32
        )
        freqs = rope_base ** (-2.0 * jnp.arange(dim // 2, dtype=jnp.float32) / dim)
        angles = positions[:, None] * freqs[None, :]
        cosine, sine = jnp.cos(angles), jnp.sin(angles)
        cosine = jnp.concatenate([cosine, cosine], axis=1)
        sine = jnp.concatenate([-sine, sine], axis=1)

    with jax.named_scope("queries"):
        query, normed = call(
            query_kernel,
            "queries",
            [
                jax.ShapeDtypeStruct((tok, own_cols), jnp.bfloat16),
                jax.ShapeDtypeStruct((tok, width), jnp.bfloat16),
            ],
            [IN_SMEM] + [IN_VMEM] * 8,
            flops=8 * tok * width * own_cols // 2,
            nbytes=16 * MIB,
            scratch=[pltpu.VMEM((tok, width), jnp.float32)],
        )(
            rank,
            blocks[0],
            blocks[1],
            far,
            far_near,
            norm_gain,
            cosine,
            sine,
            held(w_query[0]),
        )

    with jax.named_scope("gather_queries"):
        queries = {0: query}
        for bits in ODD:
            queries[bits] = swapped(query, bits)
    with jax.named_scope("new_tokens"):
        heads, ctx = key_cache.shape[2], key_cache.shape[1]
        values, summed, stats = call(
            lambda *refs: new_kernel(scale, *refs),
            "new_tokens",
            [
                jax.ShapeDtypeStruct((heads, dim, ctx), jnp.bfloat16),
                jax.ShapeDtypeStruct((dim, tok * own_cols // dim), jnp.float32),
                jax.ShapeDtypeStruct((8, tok * own_cols // dim), jnp.float32),
            ],
            [IN_VMEM] * 7,
            flops=64 * tok * width * dim,
            nbytes=13 * MIB,
        )(
            query,
            normed,
            held(key_projection[0]),
            held(value_projection[0]),
            cosine,
            sine,
            held(cached_value_rows[0]),
        )

    with jax.named_scope("cache_near"):
        near_own, near_sent = cache_part(
            scale, (0, 1), rank, mask, [queries[0], queries[1]], keys, values, "cache_near"
        )
        near_got = swapped(near_sent, 1)
    with jax.named_scope("gather_queries"):
        far_odd = joined_after([queries[bits] for bits in ODD[1:]], [near_own], "join_queries")
        far_even = swapped(far_odd, 1)
    with jax.named_scope("cache_odd"):
        (odd,) = cache_part(scale, ODD[1:], rank, mask, [far_odd], keys, values, "cache_odd")
        odd_got = swapped(odd, 1)
    with jax.named_scope("cache_even"):
        (even,) = cache_part(scale, EVEN[1:], rank, mask, [far_even], keys, values, "cache_even")
    with jax.named_scope("merge_cores"):
        cols = even.shape[2]
        kept, *sent = call(
            merge_kernel,
            "merge_cores",
            [jax.ShapeDtypeStruct((dim + 8, cols), jnp.float32)]
            + [jax.ShapeDtypeStruct((dim + 16, cols), jnp.bfloat16)] * 3,
            [IN_VMEM] * 4,
            nbytes=2 * MIB,
        )(near_own, even, near_got, odd_got)
    with jax.named_scope("exchange_parts"):
        parts = [swapped(block, bits) for block, bits in zip(sent, SAME_CORE)]
    with jax.named_scope("project"):
        own, other = call(
            output_kernel,
            "project",
            [
                jax.ShapeDtypeStruct((tok // 2, width), jnp.float32),
                jax.ShapeDtypeStruct((tok // 2, width), jnp.bfloat16),
            ],
            [IN_SMEM] + [IN_VMEM] * 7,
            flops=8 * tok * width * own_cols // 2,
            nbytes=18 * MIB,
            scratch=[
                pltpu.VMEM((tok, own_cols), jnp.float32),
                pltpu.VMEM((tok, own_cols), jnp.bfloat16),
            ],
        )(rank, kept, *parts, summed, stats, held(w_out[0]))
    with jax.named_scope("reduce_cores"):
        pair = own + swapped(other, 1).astype(jnp.float32)
    with jax.named_scope("reduce_chips"):
        total = tokens[0].astype(jnp.float32) + pair[:count]
        for i, bits in enumerate(SAME_CORE):
            block = pair[(i + 1) * count : (i + 2) * count].astype(jnp.bfloat16)
            total = total + swapped(block, bits).astype(jnp.float32)
        layer_out = total.astype(jnp.bfloat16)
    with jax.named_scope("hand_on"):
        handed = passed_along(layer_out, "section", 1)
    return handed[None]


def on_device(*arrays):
    tokens, w_query, key_projection, key_cache = arrays[0], arrays[2], arrays[3], arrays[6]
    head_dim = key_cache.shape[3]
    kv_heads = key_cache.shape[2]
    n_seq = lax.axis_size("seq")
    tok_all = tokens.shape[1] * n_seq
    if (
        n_seq == kv_heads == 8
        and key_projection.shape[2] == head_dim == 128
        and tokens.shape[1] == 8
        and tok_all == 2 * QB
    ):
        return on_device_owned(*arrays)
    return on_device_any(*arrays)


def solution(mesh):
    placed = (
        P("section", "seq", None),
        P("section", None),
        P("section", None, "seq"),
        P("section", None, "seq"),
        P("section", None, "seq"),
        P("section", "seq", None),
        P("section", "seq", None, None),
        P("section", "seq", None, None),
        P("section", None, "seq"),
        P("section"),
    )
    return jax.shard_map(
        on_device, mesh=mesh, in_specs=placed, out_specs=P("section", "seq", None), check_vma=False
    )
```

```python
import jax
import jax.numpy as jnp
from jax import lax
from jax.experimental import pallas as pl
from jax.experimental.pallas import tpu as pltpu
from jax.sharding import PartitionSpec as P

QB = 32
KB = 128


rope_base = 500000.0
neg_fill = -1e30
norm_eps = 1e-05


def passed_along(block, axis, distance):
    devices = range(lax.axis_size(axis))
    route = [((i - distance) % len(devices), i) for i in devices]
    return lax.ppermute(block, axis, route)


def apply_rotation(values, token_positions):
    half = values.shape[-1] // 2
    freqs = rope_base ** (-2.0 * jnp.arange(half, dtype=jnp.float32) / values.shape[-1])
    angles = token_positions[:, None] * freqs[None, :]
    cosine = jnp.cos(angles)[:, None, :]
    sine = jnp.sin(angles)[:, None, :]
    first = values[..., :half]
    second = values[..., half:]
    return jnp.concatenate(
        [first * cosine - second * sine, second * cosine + first * sine], axis=-1
    )


def on_device_any(
    tokens,
    norm_gain,
    w_query,
    key_projection,
    value_projection,
    w_out,
    key_cache,
    cached_value_rows,
    cache_mask,
    span_offset,
):
    n_seq = lax.axis_size("seq")
    rank = lax.axis_index("seq")
    head_dim = key_cache.shape[3]
    kv_heads = key_cache.shape[2]
    own_heads = w_query.shape[2] // head_dim
    all_heads = own_heads * n_seq
    group = all_heads // kv_heads
    tok_local = tokens.shape[1]
    tok_all = tok_local * n_seq
    ctx_local = key_cache.shape[1]
    scale = head_dim ** (-0.5)
    query_cols = own_heads * head_dim
    key_cols = key_projection.shape[2]
    offset = span_offset[0].astype(jnp.float32)
    resid = tokens[0].astype(jnp.float32)
    mean_square = jnp.mean(resid * resid, axis=-1, keepdims=True)
    input_normalized = (
        resid * lax.rsqrt(mean_square + norm_eps) * norm_gain[0].astype(jnp.float32)
    ).astype(jnp.bfloat16)
    piece = lax.all_gather(input_normalized, "seq", axis=0, tiled=True)
    rows = piece.shape[0]
    token_positions = offset + jnp.arange(rows, dtype=jnp.int32).astype(jnp.float32)
    query = jnp.dot(piece, w_query[0], preferred_element_type=jnp.float32)
    query = apply_rotation(query.reshape(rows, own_heads, head_dim), token_positions).reshape(
        rows, query_cols
    )
    key_unrotated = jnp.dot(piece, key_projection[0], preferred_element_type=jnp.float32)
    value_raw = jnp.dot(piece, value_projection[0], preferred_element_type=jnp.float32)
    fresh = jnp.concatenate([query, key_unrotated, value_raw], axis=1).astype(jnp.bfloat16)
    own_query = fresh[:, :query_cols]
    query_all, key_all, value_all = (
        lax.all_gather(own_query, "seq", axis=1, tiled=True),
        lax.all_gather(fresh[:, query_cols : query_cols + key_cols], "seq", axis=1, tiled=True),
        lax.all_gather(fresh[:, query_cols + key_cols :], "seq", axis=1, tiled=True),
    )
    positions_all = offset + jnp.arange(tok_all, dtype=jnp.int32).astype(jnp.float32)
    key_rot = apply_rotation(
        key_all.astype(jnp.float32).reshape(tok_all, kv_heads, head_dim), positions_all
    ).astype(jnp.bfloat16)
    value_heads = value_all.reshape(tok_all, kv_heads, head_dim)
    query_grouped = query_all.reshape(tok_all, kv_heads, group, head_dim)
    block = min(512, ctx_local)
    per_block = block // KB
    q_blocks = tok_all // QB

    def cache_step(index, carry):
        top, total, summed = carry
        keys = lax.dynamic_slice_in_dim(key_cache[0], index * block, block, 0)
        values = lax.dynamic_slice_in_dim(cached_value_rows[0], index * block, block, 0)
        visible = lax.dynamic_slice_in_dim(cache_mask[0], index * per_block, per_block, 1) > 0
        scores = (
            jnp.einsum("tgjd,cgd->tgjc", query_grouped, keys, preferred_element_type=jnp.float32)
            * scale
        )
        shaped = scores.reshape(q_blocks, QB, kv_heads, group, per_block, KB)
        allowed = visible[:, None, None, None, :, None]
        shaped = jnp.where(allowed, shaped, neg_fill)
        block_top = jnp.max(shaped, axis=(4, 5)).reshape(tok_all, kv_heads, group)
        new_top = jnp.maximum(top, block_top)
        lifted = new_top.reshape(q_blocks, QB, kv_heads, group, 1, 1)
        weights = jnp.where(allowed, jnp.exp(shaped - lifted), 0.0).reshape(
            tok_all, kv_heads, group, block
        )
        factor = jnp.exp(top - new_top)
        total = total * factor + jnp.sum(weights, axis=-1)
        summed = summed * factor[..., None] + jnp.einsum(
            "tgjc,cgd->tgjd",
            weights.astype(jnp.bfloat16),
            values,
            preferred_element_type=jnp.float32,
        )
        return (new_top, total, summed)

    start_top = jnp.full((tok_all, kv_heads, group), neg_fill, jnp.float32)
    start_total = jnp.zeros((tok_all, kv_heads, group), jnp.float32)
    start_sum = jnp.zeros((tok_all, kv_heads, group, head_dim), jnp.float32)
    top, total, summed = lax.fori_loop(
        0, ctx_local // block, cache_step, (start_top, start_total, start_sum)
    )
    top = top.reshape(tok_all, all_heads)
    total = total.reshape(tok_all, all_heads)
    summed = summed.reshape(tok_all, all_heads, head_dim)
    got_sum, got_top, got_total = (
        lax.all_to_all(summed[None], "seq", split_axis=2, concat_axis=0, tiled=True),
        lax.all_to_all(top[None], "seq", split_axis=2, concat_axis=0, tiled=True),
        lax.all_to_all(total[None], "seq", split_axis=2, concat_axis=0, tiled=True),
    )
    cache_top = jnp.max(got_top, axis=0)
    factor = jnp.exp(got_top - cache_top[None])
    cache_total = jnp.sum(got_total * factor, axis=0)
    cache_sum = jnp.sum(got_sum * factor[..., None], axis=0)
    kv_index = (rank * own_heads + jnp.arange(own_heads, dtype=jnp.int32)) // group
    own_keys = jnp.take(key_rot, kv_index, axis=1)
    own_values = jnp.take(value_heads, kv_index, axis=1)
    own_q = own_query.reshape(tok_all, own_heads, head_dim)
    self_scores = (
        jnp.einsum("thd,shd->ths", own_q, own_keys, preferred_element_type=jnp.float32) * scale
    )
    row_ids = jnp.arange(tok_all, dtype=jnp.int32)
    causal = (row_ids[None, :] <= row_ids[:, None])[:, None, :]
    self_scores = jnp.where(causal, self_scores, neg_fill)
    top_all = jnp.maximum(cache_top, jnp.max(self_scores, axis=-1))
    cache_factor = jnp.exp(cache_top - top_all)
    self_weights = jnp.where(causal, jnp.exp(self_scores - top_all[..., None]), 0.0)
    total_all = cache_total * cache_factor + jnp.sum(self_weights, axis=-1)
    sum_all = cache_sum * cache_factor[..., None] + jnp.einsum(
        "ths,shd->thd",
        self_weights.astype(jnp.bfloat16),
        own_values,
        preferred_element_type=jnp.float32,
    )
    attention = (sum_all / total_all[..., None]).reshape(tok_all, query_cols).astype(jnp.bfloat16)
    projected = lax.psum_scatter(
        jnp.dot(attention, w_out[0], preferred_element_type=jnp.float32).astype(jnp.bfloat16),
        "seq",
        scatter_dimension=0,
        tiled=True,
    ).astype(jnp.float32)
    layer_out = (resid + projected).astype(jnp.bfloat16)
    handed = passed_along(layer_out, "section", 1)
    return handed[None]


MIB = 1 << 20
log2e = 1.4426950408889634
IN_VMEM = pl.BlockSpec(memory_space=pltpu.VMEM)
IN_SMEM = pl.BlockSpec(memory_space=pltpu.SMEM)
SAME_CORE = (2, 4, 6)
EVEN = (0, 2, 4, 6)
ODD = (1, 3, 5, 7)


def swapped(block, bits):
    n = lax.axis_size("seq")
    return lax.ppermute(block, "seq", [(i, i ^ bits) for i in range(n)])


def onward(block, bits):
    sections, n = lax.axis_size("section"), lax.axis_size("seq")
    route = [
        (s * n + i, (s + 1) % sections * n + (i ^ bits)) for s in range(sections) for i in range(n)
    ]
    return lax.ppermute(block, ("section", "seq"), route)


def call(kernel, name, out_shape, in_specs, flops=0, nbytes=0, scratch=(), vmem=6, **grid):
    out_specs = grid.pop("out_specs", jax.tree.map(lambda _: IN_VMEM, out_shape))
    return pl.pallas_call(
        kernel,
        out_shape=out_shape,
        in_specs=in_specs,
        out_specs=out_specs,
        scratch_shapes=list(scratch),
        name=name,
        cost_estimate=pl.CostEstimate(flops=flops, bytes_accessed=nbytes, transcendentals=0),
        compiler_params=pltpu.CompilerParams(vmem_limit_bytes=vmem * MIB),
        **grid,
    )


def held(array):
    return pltpu.with_memory_space_constraint(array, pltpu.VMEM)


def join_kernel(count, *refs):
    for i in range(count):
        refs[-1][i] = refs[i][...]


def joined_after(blocks, done, name):
    count = len(blocks)
    return call(
        lambda *refs: join_kernel(count, *refs),
        name,
        jax.ShapeDtypeStruct((count, *blocks[0].shape), blocks[0].dtype),
        [IN_VMEM] * count + [pl.BlockSpec(memory_space=pl.ANY)] * len(done),
        nbytes=MIB,
        vmem=2,
    )(*blocks, *done)


def rotated(heads, cosine, sine):
    half = heads.shape[1] // 2
    return heads * cosine + pltpu.roll(heads, half, 1) * sine


def query_kernel(rank, *refs):
    same_core, other_core, gain, cosine, sine, weights, query, normed, rows = refs
    width = rows.shape[1]
    count = same_core.shape[1]
    blocks = [part.at[i] for i in range(4) for part in (same_core, other_core)]
    step = 1024
    for bits in range(8):
        at = pl.multiple_of((rank[0] ^ bits) * count, count)
        rows[pl.ds(at, count), :] = blocks[bits][...].astype(jnp.float32)
    squares = jnp.zeros((rows.shape[0], 128), jnp.float32)
    for c in range(0, width, 128):
        part = rows[:, c : c + 128]
        squares = squares + part * part
    mean_square = jnp.sum(squares, axis=-1, keepdims=True) / width
    factor = lax.rsqrt(mean_square + norm_eps)
    for c in range(0, width, step):
        normed[:, c : c + step] = (
            rows[:, c : c + step] * factor * gain[:, c : c + step].astype(jnp.float32)
        ).astype(jnp.bfloat16)
    dim = cosine.shape[1]
    for c in range(0, weights.shape[1], 2 * dim):
        raw = jnp.dot(
            normed[...], weights[:, c : c + 2 * dim], preferred_element_type=jnp.float32
        )
        for d in range(0, 2 * dim, dim):
            query[:, c + d : c + d + dim] = rotated(
                raw[:, d : d + dim], cosine[...], sine[...]
            ).astype(jnp.bfloat16)


def query_rows(query, q_block, heads, dim):
    rows = slice(q_block * QB, (q_block + 1) * QB)
    return jnp.concatenate([query[rows, j * dim : (j + 1) * dim] for j in range(heads)], axis=0)


def matmul_nt(a, b):
    return lax.dot_general(a, b, (((1,), (1,)), ((), ())), preferred_element_type=jnp.float32)


def by_head_kernel(rank, keys, values, keys_out, values_out, done, keys_in, values_in, sems):
    block = keys.shape[0] // sems.shape[1]
    copies = []
    for i in range(sems.shape[1]):
        at = pl.ds(i * block, block)
        copies.append(
            [
                pltpu.make_async_copy(source.at[at], target.at[at], sems.at[which, i])
                for which, (source, target) in enumerate([(keys, keys_in), (values, values_in)])
            ]
        )
    for pair in copies:
        for copy in pair:
            copy.start()
    done[...] = jnp.zeros_like(done)
    for i, pair in enumerate(copies):
        at = pl.ds(i * block, block)
        pair[0].wait()
        keys_out[:, at, :] = jnp.swapaxes(keys_in[at], 0, 1)
        pair[1].wait()
        turned = jnp.swapaxes(values_in[at], 0, 1)
        for g in range(turned.shape[0]):
            values_out[g, :, at] = turned[g].T


def cache_by_head(rank, keys, values):
    ctx, heads, dim = keys.shape
    blocks = 8
    in_hbm = pl.BlockSpec(memory_space=pltpu.HBM)
    return call(
        by_head_kernel,
        "cache_by_head",
        [
            jax.ShapeDtypeStruct((heads, ctx, dim), jnp.bfloat16),
            jax.ShapeDtypeStruct((heads, dim, ctx), jnp.bfloat16),
            jax.ShapeDtypeStruct((8, 128), jnp.float32),
        ],
        [IN_SMEM, in_hbm, in_hbm],
        flops=10**10,
        nbytes=ctx * heads * dim * 2,
        scratch=[
            pltpu.VMEM(keys.shape, jnp.bfloat16),
            pltpu.VMEM(values.shape, jnp.bfloat16),
            pltpu.SemaphoreType.DMA((2, blocks)),
        ],
        vmem=14,
    )(
        rank,
        pltpu.with_memory_space_constraint(keys, pltpu.HBM),
        pltpu.with_memory_space_constraint(values, pltpu.HBM),
    )


def new_kernel(
    scale,
    query,
    normed,
    w_key,
    w_value,
    cosine,
    sine,
    summed,
    stats,
):
    tok, dim = cosine.shape
    heads = query.shape[1] // dim
    raw = jnp.dot(normed[...], w_key[...], preferred_element_type=jnp.float32)
    raw = raw.astype(jnp.bfloat16).astype(jnp.float32)
    keys = rotated(raw, cosine[...], sine[...]).astype(jnp.bfloat16)
    values = jnp.dot(normed[...], w_value[...], preferred_element_type=jnp.float32)
    values = values.astype(jnp.bfloat16).astype(jnp.float32).T.astype(jnp.bfloat16)
    cols = heads * QB
    for q_block in range(tok // QB):
        scores = matmul_nt(keys, query_rows(query, q_block, heads, dim)) * scale
        u = lax.broadcasted_iota(jnp.int32, (tok, cols), 0)
        t = lax.broadcasted_iota(jnp.int32, (tok, cols), 1) % QB + q_block * QB
        allowed = u <= t
        scores = jnp.where(allowed, scores, neg_fill)
        top = jnp.max(scores, axis=0, keepdims=True)
        weights = jnp.where(allowed, jnp.exp2(scores - top), 0.0)
        at = slice(q_block * cols, (q_block + 1) * cols)
        stats[0:1, at] = top
        stats[1:2, at] = jnp.sum(weights, axis=0, keepdims=True)
        summed[:, at] = jnp.dot(
            values, weights.astype(jnp.bfloat16), preferred_element_type=jnp.float32
        )


def split_rows(level, rows):
    high = level.astype(jnp.bfloat16).astype(jnp.float32)
    rest = level - high
    middle = rest.astype(jnp.bfloat16).astype(jnp.float32)
    low = rest - middle
    row = lax.broadcasted_iota(jnp.int32, (rows, level.shape[1]), 0)
    return jnp.where(row == 0, high, jnp.where(row == 1, middle, jnp.where(row == 2, low, 0.0)))


def level_of(tail):
    tail = tail.astype(jnp.float32)
    return tail[0:1] + tail[1:2] + tail[2:3]


def cache_kernel(scale, order, rank, mask, *refs):
    n = len(order)
    given = 1 if len(refs[0].shape) == 3 else n
    queries, (keys, values), outs = refs[:given], refs[given : given + 2], refs[given + 2 : -4]
    if given < n:
        queries = [queries[0].at[i] for i in range(n)]
    q_rows, summed, visible, scores = refs[-4:]
    dim = keys.shape[2]
    heads = queries[0].shape[1] // dim
    cols = heads * QB
    groups = [rank[0] ^ bits for bits in order]
    own = [bits for bits in order if bits in EVEN]
    for q_block in range(mask.shape[0]):
        count = jnp.int32(0)
        for b in range(mask.shape[1]):
            visible[count] = b
            count = count + (mask[q_block, b] > 0).astype(jnp.int32)
        for e in range(4):
            visible[count + e] = 0
        for i in range(n):
            q_rows[i] = query_rows(queries[i], q_block, heads, dim)
            summed[i] = jnp.zeros((dim, cols), jnp.float32)

        def places(pair):
            return [pl.multiple_of(visible[2 * pair + e] * KB, KB) for e in range(2)]

        def score(pair):
            at = places(pair)
            hidden = jnp.where(2 * pair + 1 < count, jnp.float32(0.0), jnp.float32(neg_fill))
            products = [
                matmul_nt(
                    jnp.concatenate([keys[g, pl.ds(a, KB), :] for a in at], axis=0), q_rows[i]
                )
                for i, g in enumerate(groups)
            ]
            tops = []
            for i in range(n):
                first = products[i][:KB] * scale
                second = products[i][KB:] * scale + hidden
                scores[i, :KB] = first
                scores[i, KB:] = second
                tops.append(jnp.max(jnp.maximum(first, second), axis=0, keepdims=True))
            return tops

        def step(pair, carry):
            levels, scaled = [], []
            for i in range(n):
                top, total, pair_top = carry[3 * i : 3 * i + 3]
                new_top = jnp.maximum(top, pair_top)
                weights = jnp.exp2(scores[i] - new_top)
                factor = jnp.exp2(top - new_top)
                total = total * factor + jnp.sum(weights, axis=0, keepdims=True)
                levels += [new_top, total]
                scaled.append((factor, weights.astype(jnp.bfloat16)))
            at = places(pair)
            products = [
                jnp.dot(
                    jnp.concatenate([values[g, :, pl.ds(a, KB)] for a in at], axis=1),
                    scaled[i][1],
                    preferred_element_type=jnp.float32,
                )
                for i, g in enumerate(groups)
            ]
            tops = score(pair + 1)
            after = []
            for i in range(n):
                summed[i] = summed[i] * scaled[i][0] + products[i]
                after += [levels[2 * i], levels[2 * i + 1], tops[i]]
            return tuple(after)

        start = []
        for top in score(0):
            start += [
                jnp.full((1, cols), neg_fill, jnp.float32),
                jnp.zeros((1, cols), jnp.float32),
                top,
            ]
        ended = lax.fori_loop(0, (count + 1) // 2, step, tuple(start))
        at = slice(q_block * cols, (q_block + 1) * cols)
        for i, bits in enumerate(order):
            top, total = ended[3 * i], ended[3 * i + 1]
            seen = total > 0.0
            safe = jnp.where(seen, total, 1.0)
            level = jnp.where(seen, top + jnp.log2(safe), neg_fill)
            if bits in EVEN:
                out, place = outs[0], own.index(bits)
            else:
                out, place = outs[-1], i - len(own)
            out[place, 0:dim, at] = (summed[i] * (1.0 / safe)).astype(out.dtype)
            out[place, dim:, at] = split_rows(level, out.shape[1] - dim).astype(out.dtype)


def cache_part(scale, order, rank, mask, queries, keys, values, name):
    heads, ctx, dim = keys.shape
    cols = (queries[0].shape[-1] // dim) * QB
    n = len(order)
    own = len([bits for bits in order if bits in EVEN])
    outs = []
    if own:
        outs.append(jax.ShapeDtypeStruct((own, dim + 8, mask.shape[0] * cols), jnp.float32))
    if n > own:
        outs.append(jax.ShapeDtypeStruct((n - own, dim + 16, mask.shape[0] * cols), jnp.bfloat16))
    return call(
        lambda *refs: cache_kernel(scale, order, *refs),
        name,
        outs,
        [IN_SMEM, IN_SMEM] + [IN_VMEM] * (len(queries) + 2),
        flops=(2 if own else 10) * n * queries[0].shape[-2] * heads * ctx * dim,
        nbytes=n * MIB,
        scratch=[
            pltpu.VMEM((n, cols, dim), jnp.bfloat16),
            pltpu.VMEM((n, dim, cols), jnp.float32),
            pltpu.SMEM((mask.shape[1] + 4,), jnp.int32),
            pltpu.VMEM((n, 2 * KB, cols), jnp.float32),
        ],
    )(rank, mask, *queries, held(keys), held(values))


def merge_kernel(own_first, own_rest, got_first, got_rest, kept, *sent):
    dim = own_first.shape[1] - 8
    for i in range(4):
        own = own_first.at[0] if i == 0 else own_rest.at[i - 1]
        got = got_first.at[0] if i == 0 else got_rest.at[i - 1]
        mine, other = level_of(own[dim:, :]), level_of(got[dim:, :])
        top = jnp.maximum(mine, other)
        mine, other = jnp.exp2(mine - top), jnp.exp2(other - top)
        total = mine + other
        level = top + jnp.log2(total)
        mine, other = mine / total, other / total
        joined = own[:dim, :] * mine + got[:dim, :].astype(jnp.float32) * other
        target = kept if i == 0 else sent[i - 1]
        target[:dim, :] = joined.astype(target.dtype)
        target[dim:, :] = split_rows(level, target.shape[0] - dim).astype(target.dtype)


def output_kernel(
    rank,
    kept,
    got_a,
    got_b,
    got_c,
    summed,
    stats,
    weights,
    own,
    sent,
    rows,
    sorted_rows,
):
    dim = summed.shape[0]
    levels = [level_of(part[dim:, :]) for part in (kept, got_a, got_b, got_c)]
    top = stats[0:1, :]
    for level in levels:
        top = jnp.maximum(top, level)
    factor = jnp.exp2(stats[0:1, :] - top)
    total = stats[1:2, :] * factor
    joined = summed[...] * factor
    for part, level in zip((kept, got_a, got_b, got_c), levels):
        factor = jnp.exp2(level - top)
        total = total + factor
        joined = joined + part[:dim, :].astype(jnp.float32) * factor
    joined = joined * (1.0 / total)
    heads = rows.shape[1] // dim
    cols = heads * QB
    for q_block in range(rows.shape[0] // QB):
        turned = joined[:, q_block * cols : (q_block + 1) * cols].T
        for j in range(heads):
            rows[q_block * QB : (q_block + 1) * QB, j * dim : (j + 1) * dim] = turned[
                j * QB : (j + 1) * QB, :
            ]
    count = rows.shape[0] // 8
    for pair in range(4):
        chunk = [
            rows[pl.ds(pl.multiple_of((rank[0] ^ bits) * count, count), count), :]
            for bits in (EVEN + ODD)[2 * pair : 2 * pair + 2]
        ]
        sorted_rows[2 * count * pair : 2 * count * (pair + 1), :] = jnp.concatenate(
            chunk, axis=0
        ).astype(jnp.bfloat16)
    half = rows.shape[0] // 2
    step = 512
    for c in range(0, weights.shape[1], step):
        product = jnp.dot(
            sorted_rows[...], weights[:, c : c + step], preferred_element_type=jnp.float32
        )
        own[:, c : c + step] = product[:half]
        sent[:, c : c + step] = product[half:].astype(jnp.bfloat16)


def on_device_owned(
    tokens,
    norm_gain,
    w_query,
    key_projection,
    value_projection,
    w_out,
    key_cache,
    cached_value_rows,
    cache_mask,
    span_offset,
):
    n_seq = lax.axis_size("seq")
    rank = lax.axis_index("seq").astype(jnp.int32)[None]
    dim = key_cache.shape[3]
    count = tokens.shape[1]
    width = tokens.shape[2]
    tok = count * n_seq
    own_cols = w_query.shape[2]
    scale = dim ** (-0.5) * log2e
    mask = cache_mask[0]

    with jax.named_scope("cache_layout"):
        keys, values, layout_done = cache_by_head(rank, key_cache[0], cached_value_rows[0])
    with jax.named_scope("gather_tokens"):
        blocks = {0: tokens[0]}
        for bits in SAME_CORE:
            blocks[bits] = swapped(blocks[0], bits)
        same_core = joined_after([blocks[bits] for bits in EVEN], [layout_done], "join_tokens")
        other_core = swapped(same_core, 1)

    with jax.named_scope("tables"):
        positions = span_offset[0].astype(jnp.float32) + jnp.arange(tok, dtype=jnp.int32).astype(
            jnp.float32
        )
        freqs = rope_base ** (-2.0 * jnp.arange(dim // 2, dtype=jnp.float32) / dim)
        angles = positions[:, None] * freqs[None, :]
        cosine, sine = jnp.cos(angles), jnp.sin(angles)
        cosine = jnp.concatenate([cosine, cosine], axis=1)
        sine = jnp.concatenate([-sine, sine], axis=1)

    with jax.named_scope("queries"):
        query, normed = call(
            query_kernel,
            "queries",
            [
                jax.ShapeDtypeStruct((tok, own_cols), jnp.bfloat16),
                jax.ShapeDtypeStruct((tok, width), jnp.bfloat16),
            ],
            [IN_SMEM] + [IN_VMEM] * 6,
            flops=8 * tok * width * own_cols // 2,
            nbytes=16 * MIB,
            scratch=[pltpu.VMEM((tok, width), jnp.float32)],
        )(
            rank,
            same_core,
            other_core,
            norm_gain,
            cosine,
            sine,
            held(w_query[0]),
        )

    with jax.named_scope("gather_queries"):
        queries = {0: query}
        for bits in ODD:
            queries[bits] = swapped(query, bits)
    with jax.named_scope("new_tokens"):
        summed, stats = call(
            lambda *refs: new_kernel(scale, *refs),
            "new_tokens",
            [
                jax.ShapeDtypeStruct((dim, tok * own_cols // dim), jnp.float32),
                jax.ShapeDtypeStruct((8, tok * own_cols // dim), jnp.float32),
            ],
            [IN_VMEM] * 6,
            flops=16 * tok * width * dim,
            nbytes=5 * MIB,
        )(
            query,
            normed,
            held(key_projection[0]),
            held(value_projection[0]),
            cosine,
            sine,
        )

    with jax.named_scope("cache_near"):
        near_own, near_sent = cache_part(
            scale, (0, 1), rank, mask, [queries[0], queries[1]], keys, values, "cache_near"
        )
        near_got = swapped(near_sent, 1)
    with jax.named_scope("gather_queries"):
        far_odd = joined_after([queries[bits] for bits in ODD[1:]], [near_own], "join_queries")
        far_even = swapped(far_odd, 1)
    with jax.named_scope("cache_odd"):
        (odd,) = cache_part(scale, ODD[1:], rank, mask, [far_odd], keys, values, "cache_odd")
        odd_got = swapped(odd, 1)
    with jax.named_scope("cache_even"):
        (even,) = cache_part(scale, EVEN[1:], rank, mask, [far_even], keys, values, "cache_even")
    with jax.named_scope("merge_cores"):
        cols = even.shape[2]
        kept, *sent = call(
            merge_kernel,
            "merge_cores",
            [jax.ShapeDtypeStruct((dim + 8, cols), jnp.float32)]
            + [jax.ShapeDtypeStruct((dim + 16, cols), jnp.bfloat16)] * 3,
            [IN_VMEM] * 4,
            nbytes=2 * MIB,
        )(near_own, even, near_got, odd_got)
    with jax.named_scope("exchange_parts"):
        parts = [swapped(block, bits) for block, bits in zip(sent, SAME_CORE)]
    with jax.named_scope("project"):
        own, other = call(
            output_kernel,
            "project",
            [
                jax.ShapeDtypeStruct((tok // 2, width), jnp.float32),
                jax.ShapeDtypeStruct((tok // 2, width), jnp.bfloat16),
            ],
            [IN_SMEM] + [IN_VMEM] * 7,
            flops=8 * tok * width * own_cols // 2,
            nbytes=18 * MIB,
            scratch=[
                pltpu.VMEM((tok, own_cols), jnp.float32),
                pltpu.VMEM((tok, own_cols), jnp.bfloat16),
            ],
        )(rank, kept, *parts, summed, stats, held(w_out[0]))
    with jax.named_scope("reduce_cores"):
        pair = own + swapped(other, 1).astype(jnp.float32)
    with jax.named_scope("reduce_on_next_section"):
        total = 0.0
        for i, bits in enumerate(EVEN):
            block = pair[i * count : (i + 1) * count]
            if bits == 0:
                block = tokens[0].astype(jnp.float32) + block
            total = total + onward(block.astype(jnp.bfloat16), bits).astype(jnp.float32)
        handed = total.astype(jnp.bfloat16)
    return handed[None]


def on_device(*arrays):
    tokens, w_query, key_projection, key_cache = arrays[0], arrays[2], arrays[3], arrays[6]
    head_dim = key_cache.shape[3]
    kv_heads = key_cache.shape[2]
    n_seq = lax.axis_size("seq")
    tok_all = tokens.shape[1] * n_seq
    if (
        n_seq == kv_heads == 8
        and key_projection.shape[2] == head_dim == 128
        and tokens.shape[1] == 8
        and tok_all == 2 * QB
    ):
        return on_device_owned(*arrays)
    return on_device_any(*arrays)


def solution(mesh):
    placed = (
        P("section", "seq", None),
        P("section", None),
        P("section", None, "seq"),
        P("section", None, "seq"),
        P("section", None, "seq"),
        P("section", "seq", None),
        P("section", "seq", None, None),
        P("section", "seq", None, None),
        P("section", None, "seq"),
        P("section"),
    )
    return jax.shard_map(
        on_device, mesh=mesh, in_specs=placed, out_specs=P("section", "seq", None), check_vma=False
    )
```

```python
import functools

import jax
import jax.numpy as jnp
from jax import lax
from jax.experimental import pallas as pl
from jax.experimental.pallas import tpu as pltpu
from jax.sharding import PartitionSpec as P

QB = 32
KB = 128


rope_base = 500000.0
neg_fill = -1e30
norm_eps = 1e-05


def passed_along(block, axis, distance):
    devices = range(lax.axis_size(axis))
    route = [((i - distance) % len(devices), i) for i in devices]
    return lax.ppermute(block, axis, route)


def apply_rotation(values, token_positions):
    half = values.shape[-1] // 2
    freqs = rope_base ** (-2.0 * jnp.arange(half, dtype=jnp.float32) / values.shape[-1])
    angles = token_positions[:, None] * freqs[None, :]
    cosine = jnp.cos(angles)[:, None, :]
    sine = jnp.sin(angles)[:, None, :]
    first = values[..., :half]
    second = values[..., half:]
    return jnp.concatenate(
        [first * cosine - second * sine, second * cosine + first * sine], axis=-1
    )


def on_device_any(
    tokens,
    norm_gain,
    w_query,
    key_projection,
    value_projection,
    w_out,
    key_cache,
    cached_value_rows,
    cache_mask,
    span_offset,
):
    n_seq = lax.axis_size("seq")
    rank = lax.axis_index("seq")
    head_dim = key_cache.shape[3]
    kv_heads = key_cache.shape[2]
    own_heads = w_query.shape[2] // head_dim
    all_heads = own_heads * n_seq
    group = all_heads // kv_heads
    tok_local = tokens.shape[1]
    tok_all = tok_local * n_seq
    ctx_local = key_cache.shape[1]
    scale = head_dim ** (-0.5)
    query_cols = own_heads * head_dim
    key_cols = key_projection.shape[2]
    offset = span_offset[0].astype(jnp.float32)
    resid = tokens[0].astype(jnp.float32)
    mean_square = jnp.mean(resid * resid, axis=-1, keepdims=True)
    input_normalized = (
        resid * lax.rsqrt(mean_square + norm_eps) * norm_gain[0].astype(jnp.float32)
    ).astype(jnp.bfloat16)
    piece = lax.all_gather(input_normalized, "seq", axis=0, tiled=True)
    rows = piece.shape[0]
    token_positions = offset + jnp.arange(rows, dtype=jnp.int32).astype(jnp.float32)
    query = jnp.dot(piece, w_query[0], preferred_element_type=jnp.float32)
    query = apply_rotation(query.reshape(rows, own_heads, head_dim), token_positions).reshape(
        rows, query_cols
    )
    key_unrotated = jnp.dot(piece, key_projection[0], preferred_element_type=jnp.float32)
    value_raw = jnp.dot(piece, value_projection[0], preferred_element_type=jnp.float32)
    fresh = jnp.concatenate([query, key_unrotated, value_raw], axis=1).astype(jnp.bfloat16)
    own_query = fresh[:, :query_cols]
    query_all, key_all, value_all = (
        lax.all_gather(own_query, "seq", axis=1, tiled=True),
        lax.all_gather(fresh[:, query_cols : query_cols + key_cols], "seq", axis=1, tiled=True),
        lax.all_gather(fresh[:, query_cols + key_cols :], "seq", axis=1, tiled=True),
    )
    positions_all = offset + jnp.arange(tok_all, dtype=jnp.int32).astype(jnp.float32)
    key_rot = apply_rotation(
        key_all.astype(jnp.float32).reshape(tok_all, kv_heads, head_dim), positions_all
    ).astype(jnp.bfloat16)
    value_heads = value_all.reshape(tok_all, kv_heads, head_dim)
    query_grouped = query_all.reshape(tok_all, kv_heads, group, head_dim)
    block = min(512, ctx_local)
    per_block = block // KB
    q_blocks = tok_all // QB

    def cache_step(index, carry):
        top, total, summed = carry
        keys = lax.dynamic_slice_in_dim(key_cache[0], index * block, block, 0)
        values = lax.dynamic_slice_in_dim(cached_value_rows[0], index * block, block, 0)
        visible = lax.dynamic_slice_in_dim(cache_mask[0], index * per_block, per_block, 1) > 0
        scores = (
            jnp.einsum("tgjd,cgd->tgjc", query_grouped, keys, preferred_element_type=jnp.float32)
            * scale
        )
        shaped = scores.reshape(q_blocks, QB, kv_heads, group, per_block, KB)
        allowed = visible[:, None, None, None, :, None]
        shaped = jnp.where(allowed, shaped, neg_fill)
        block_top = jnp.max(shaped, axis=(4, 5)).reshape(tok_all, kv_heads, group)
        new_top = jnp.maximum(top, block_top)
        lifted = new_top.reshape(q_blocks, QB, kv_heads, group, 1, 1)
        weights = jnp.where(allowed, jnp.exp(shaped - lifted), 0.0).reshape(
            tok_all, kv_heads, group, block
        )
        factor = jnp.exp(top - new_top)
        total = total * factor + jnp.sum(weights, axis=-1)
        summed = summed * factor[..., None] + jnp.einsum(
            "tgjc,cgd->tgjd",
            weights.astype(jnp.bfloat16),
            values,
            preferred_element_type=jnp.float32,
        )
        return (new_top, total, summed)

    start_top = jnp.full((tok_all, kv_heads, group), neg_fill, jnp.float32)
    start_total = jnp.zeros((tok_all, kv_heads, group), jnp.float32)
    start_sum = jnp.zeros((tok_all, kv_heads, group, head_dim), jnp.float32)
    top, total, summed = lax.fori_loop(
        0, ctx_local // block, cache_step, (start_top, start_total, start_sum)
    )
    top = top.reshape(tok_all, all_heads)
    total = total.reshape(tok_all, all_heads)
    summed = summed.reshape(tok_all, all_heads, head_dim)
    got_sum, got_top, got_total = (
        lax.all_to_all(summed[None], "seq", split_axis=2, concat_axis=0, tiled=True),
        lax.all_to_all(top[None], "seq", split_axis=2, concat_axis=0, tiled=True),
        lax.all_to_all(total[None], "seq", split_axis=2, concat_axis=0, tiled=True),
    )
    cache_top = jnp.max(got_top, axis=0)
    factor = jnp.exp(got_top - cache_top[None])
    cache_total = jnp.sum(got_total * factor, axis=0)
    cache_sum = jnp.sum(got_sum * factor[..., None], axis=0)
    kv_index = (rank * own_heads + jnp.arange(own_heads, dtype=jnp.int32)) // group
    own_keys = jnp.take(key_rot, kv_index, axis=1)
    own_values = jnp.take(value_heads, kv_index, axis=1)
    own_q = own_query.reshape(tok_all, own_heads, head_dim)
    self_scores = (
        jnp.einsum("thd,shd->ths", own_q, own_keys, preferred_element_type=jnp.float32) * scale
    )
    row_ids = jnp.arange(tok_all, dtype=jnp.int32)
    causal = (row_ids[None, :] <= row_ids[:, None])[:, None, :]
    self_scores = jnp.where(causal, self_scores, neg_fill)
    top_all = jnp.maximum(cache_top, jnp.max(self_scores, axis=-1))
    cache_factor = jnp.exp(cache_top - top_all)
    self_weights = jnp.where(causal, jnp.exp(self_scores - top_all[..., None]), 0.0)
    total_all = cache_total * cache_factor + jnp.sum(self_weights, axis=-1)
    sum_all = cache_sum * cache_factor[..., None] + jnp.einsum(
        "ths,shd->thd",
        self_weights.astype(jnp.bfloat16),
        own_values,
        preferred_element_type=jnp.float32,
    )
    attention = (sum_all / total_all[..., None]).reshape(tok_all, query_cols).astype(jnp.bfloat16)
    projected = lax.psum_scatter(
        jnp.dot(attention, w_out[0], preferred_element_type=jnp.float32).astype(jnp.bfloat16),
        "seq",
        scatter_dimension=0,
        tiled=True,
    ).astype(jnp.float32)
    layer_out = (resid + projected).astype(jnp.bfloat16)
    handed = passed_along(layer_out, "section", 1)
    return handed[None]


MIB = 1 << 20
log2e = 1.4426950408889634
IN_VMEM = pl.BlockSpec(memory_space=pltpu.VMEM)
IN_SMEM = pl.BlockSpec(memory_space=pltpu.SMEM)
SAME_CORE = (2, 4, 6)
EVEN = (0, 2, 4, 6)
ODD = (1, 3, 5, 7)


def swapped(block, bits):
    n = lax.axis_size("seq")
    return lax.ppermute(block, "seq", [(i, i ^ bits) for i in range(n)])


def onward(block, bits):
    sections, n = lax.axis_size("section"), lax.axis_size("seq")
    route = [
        (s * n + i, (s + 1) % sections * n + (i ^ bits)) for s in range(sections) for i in range(n)
    ]
    return lax.ppermute(block, ("section", "seq"), route)


def call(kernel, name, out_shape, in_specs, flops=0, nbytes=0, scratch=(), vmem=6, **grid):
    out_specs = grid.pop("out_specs", jax.tree.map(lambda _: IN_VMEM, out_shape))
    return pl.pallas_call(
        kernel,
        out_shape=out_shape,
        in_specs=in_specs,
        out_specs=out_specs,
        scratch_shapes=list(scratch),
        name=name,
        cost_estimate=pl.CostEstimate(flops=flops, bytes_accessed=nbytes, transcendentals=0),
        compiler_params=pltpu.CompilerParams(vmem_limit_bytes=vmem * MIB),
        **grid,
    )


def held(array):
    return pltpu.with_memory_space_constraint(array, pltpu.VMEM)


def join_kernel(count, *refs):
    for i in range(count):
        refs[-1][i] = refs[i][...]


def joined_after(blocks, done, name):
    count = len(blocks)
    return call(
        lambda *refs: join_kernel(count, *refs),
        name,
        jax.ShapeDtypeStruct((count, *blocks[0].shape), blocks[0].dtype),
        [IN_VMEM] * count + [pl.BlockSpec(memory_space=pl.ANY)] * len(done),
        nbytes=MIB,
        vmem=2,
    )(*blocks, *done)


def rotated(heads, cosine, sine):
    half = heads.shape[1] // 2
    return heads * cosine + pltpu.roll(heads, half, 1) * sine


def query_kernel(rank, *refs):
    same_core, other_core, gain, cosine, sine, weights, query, normed, rows = refs
    width = rows.shape[1]
    count = same_core.shape[1]
    blocks = [part.at[i] for i in range(4) for part in (same_core, other_core)]
    step = 1024
    for bits in range(8):
        at = pl.multiple_of((rank[0] ^ bits) * count, count)
        rows[pl.ds(at, count), :] = blocks[bits][...].astype(jnp.float32)
    squares = jnp.zeros((rows.shape[0], 128), jnp.float32)
    for c in range(0, width, 128):
        part = rows[:, c : c + 128]
        squares = squares + part * part
    mean_square = jnp.sum(squares, axis=-1, keepdims=True) / width
    factor = lax.rsqrt(mean_square + norm_eps)
    for c in range(0, width, step):
        normed[:, c : c + step] = (
            rows[:, c : c + step] * factor * gain[:, c : c + step].astype(jnp.float32)
        ).astype(jnp.bfloat16)
    dim = cosine.shape[1]
    for c in range(0, weights.shape[1], 2 * dim):
        raw = jnp.dot(
            normed[...], weights[:, c : c + 2 * dim], preferred_element_type=jnp.float32
        )
        for d in range(0, 2 * dim, dim):
            query[:, c + d : c + d + dim] = rotated(
                raw[:, d : d + dim], cosine[...], sine[...]
            ).astype(jnp.bfloat16)


def query_rows(query, q_block, heads, dim):
    rows = slice(q_block * QB, (q_block + 1) * QB)
    return jnp.concatenate([query[rows, j * dim : (j + 1) * dim] for j in range(heads)], axis=0)


def matmul_nt(a, b):
    return lax.dot_general(a, b, (((1,), (1,)), ((), ())), preferred_element_type=jnp.float32)


def by_head_kernel(rank, keys, values, keys_out, values_out, done, keys_in, values_in, sems):
    blocks = sems.shape[1]
    block = keys.shape[0] // blocks

    def copies(i):
        at = pl.ds(pl.multiple_of(i * block, block), block)
        return [
            pltpu.make_async_copy(source.at[at], target.at[at], sems.at[which, i])
            for which, (source, target) in enumerate([(keys, keys_in), (values, values_in)])
        ]

    @pl.loop(0, blocks)
    def _(i):
        for copy in copies(i):
            copy.start()

    done[...] = jnp.zeros_like(done)

    @pl.loop(0, blocks)
    def _(i):
        at = pl.ds(pl.multiple_of(i * block, block), block)
        for copy in copies(i):
            copy.wait()
        keys_out[:, at, :] = jnp.swapaxes(keys_in[at], 0, 1)
        turned = jnp.swapaxes(values_in[at], 0, 1)
        for g in range(turned.shape[0]):
            values_out[g, :, at] = turned[g].T


def cache_by_head(rank, keys, values):
    ctx, heads, dim = keys.shape
    blocks = 8
    in_hbm = pl.BlockSpec(memory_space=pltpu.HBM)
    return call(
        by_head_kernel,
        "cache_by_head",
        [
            jax.ShapeDtypeStruct((heads, ctx, dim), jnp.bfloat16),
            jax.ShapeDtypeStruct((heads, dim, ctx), jnp.bfloat16),
            jax.ShapeDtypeStruct((8, 128), jnp.float32),
        ],
        [IN_SMEM, in_hbm, in_hbm],
        flops=10**10,
        nbytes=ctx * heads * dim * 2,
        scratch=[
            pltpu.VMEM(keys.shape, jnp.bfloat16),
            pltpu.VMEM(values.shape, jnp.bfloat16),
            pltpu.SemaphoreType.DMA((2, blocks)),
        ],
        vmem=14,
    )(
        rank,
        pltpu.with_memory_space_constraint(keys, pltpu.HBM),
        pltpu.with_memory_space_constraint(values, pltpu.HBM),
    )


def new_kernel(
    scale,
    query,
    normed,
    w_key,
    w_value,
    cosine,
    sine,
    summed,
    stats,
):
    tok, dim = cosine.shape
    heads = query.shape[1] // dim
    raw = jnp.dot(normed[...], w_key[...], preferred_element_type=jnp.float32)
    raw = raw.astype(jnp.bfloat16).astype(jnp.float32)
    keys = rotated(raw, cosine[...], sine[...]).astype(jnp.bfloat16)
    values = jnp.dot(normed[...], w_value[...], preferred_element_type=jnp.float32)
    values = values.astype(jnp.bfloat16).astype(jnp.float32).T.astype(jnp.bfloat16)
    cols = heads * QB
    for q_block in range(tok // QB):
        scores = matmul_nt(keys, query_rows(query, q_block, heads, dim)) * scale
        u = lax.broadcasted_iota(jnp.int32, (tok, cols), 0)
        t = lax.broadcasted_iota(jnp.int32, (tok, cols), 1) % QB + q_block * QB
        allowed = u <= t
        scores = jnp.where(allowed, scores, neg_fill)
        top = jnp.max(scores, axis=0, keepdims=True)
        weights = jnp.where(allowed, jnp.exp2(scores - top), 0.0)
        at = slice(q_block * cols, (q_block + 1) * cols)
        stats[0:1, at] = top
        stats[1:2, at] = jnp.sum(weights, axis=0, keepdims=True)
        summed[:, at] = jnp.dot(
            values, weights.astype(jnp.bfloat16), preferred_element_type=jnp.float32
        )


def split_rows(level, rows):
    high = level.astype(jnp.bfloat16).astype(jnp.float32)
    rest = level - high
    middle = rest.astype(jnp.bfloat16).astype(jnp.float32)
    low = rest - middle
    row = lax.broadcasted_iota(jnp.int32, (rows, level.shape[1]), 0)
    return jnp.where(row == 0, high, jnp.where(row == 1, middle, jnp.where(row == 2, low, 0.0)))


def level_of(tail):
    tail = tail.astype(jnp.float32)
    return tail[0:1] + tail[1:2] + tail[2:3]


def cache_kernel(scale, order, rank, mask, *refs):
    n = len(order)
    given = 1 if len(refs[0].shape) == 3 else n
    queries, (keys, values), outs = refs[:given], refs[given : given + 2], refs[given + 2 : -5]
    if given < n:
        queries = [queries[0].at[i] for i in range(n)]
    q_rows, summed, visible, scores, levels = refs[-5:]
    dim = keys.shape[2]
    heads = queries[0].shape[1] // dim
    cols = heads * QB
    groups = [rank[0] ^ bits for bits in order]
    own = [bits for bits in order if bits in EVEN]
    blocks = mask.shape[0]
    place = jnp.int32(0)
    ends, singles = [], []
    for q_block in range(blocks):
        for b in range(mask.shape[1]):
            visible[place] = b
            place = place + (mask[q_block, b] > 0).astype(jnp.int32)
        visible[place] = 0
        odd = place % 2
        place = place + odd
        ends.append(place // 2)
        singles.append(jnp.where(odd == 1, place // 2 - 1, -1))
        for i in range(n):
            q_rows[q_block, i] = query_rows(queries[i], q_block, heads, dim)
            summed[q_block, i] = jnp.zeros((dim, cols), jnp.float32)
            levels[q_block, i, 0:1] = jnp.full((1, cols), neg_fill, jnp.float32)
            levels[q_block, i, 1:2] = jnp.zeros((1, cols), jnp.float32)
    for e in range(2):
        visible[place + e] = 0

    def q_block_of(pair):
        return sum((pair >= end).astype(jnp.int32) for end in ends[:-1])

    def places(pair):
        return [pl.multiple_of(visible[2 * pair + e] * KB, KB) for e in range(2)]

    def score(pair):
        at = places(pair)
        q_block = q_block_of(pair)
        single = functools.reduce(jnp.logical_or, [pair == one for one in singles])
        hidden = jnp.where(single, jnp.float32(neg_fill), jnp.float32(0.0))
        products = [
            matmul_nt(
                jnp.concatenate([keys[g, pl.ds(a, KB), :] for a in at], axis=0),
                q_rows[q_block, i],
            )
            for i, g in enumerate(groups)
        ]
        tops = []
        for i in range(n):
            first = products[i][:KB] * scale
            second = products[i][KB:] * scale + hidden
            scores[i, :KB] = first
            scores[i, KB:] = second
            tops.append(jnp.max(jnp.maximum(first, second), axis=0, keepdims=True))
        return tops

    def step(pair, tops):
        q_block = q_block_of(pair)
        scaled = []
        for i in range(n):
            top, total = levels[q_block, i, 0:1], levels[q_block, i, 1:2]
            new_top = jnp.maximum(top, tops[i])
            weights = jnp.exp2(scores[i] - new_top)
            factor = jnp.exp2(top - new_top)
            levels[q_block, i, 0:1] = new_top
            levels[q_block, i, 1:2] = total * factor + jnp.sum(weights, axis=0, keepdims=True)
            scaled.append((factor, weights.astype(jnp.bfloat16)))
        at = places(pair)
        products = [
            jnp.dot(
                jnp.concatenate([values[g, :, pl.ds(a, KB)] for a in at], axis=1),
                scaled[i][1],
                preferred_element_type=jnp.float32,
            )
            for i, g in enumerate(groups)
        ]
        tops = score(pair + 1)
        for i in range(n):
            summed[q_block, i] = summed[q_block, i] * scaled[i][0] + products[i]
        return tuple(tops)

    lax.fori_loop(0, ends[-1], step, tuple(score(jnp.int32(0))))
    for q_block in range(blocks):
        at = slice(q_block * cols, (q_block + 1) * cols)
        for i, bits in enumerate(order):
            top, total = levels[q_block, i, 0:1], levels[q_block, i, 1:2]
            seen = total > 0.0
            safe = jnp.where(seen, total, 1.0)
            level = jnp.where(seen, top + jnp.log2(safe), neg_fill)
            if bits in EVEN:
                out, place = outs[0], own.index(bits)
            else:
                out, place = outs[-1], i - len(own)
            out[place, 0:dim, at] = (summed[q_block, i] * (1.0 / safe)).astype(out.dtype)
            out[place, dim:, at] = split_rows(level, out.shape[1] - dim).astype(out.dtype)


def cache_part(scale, order, rank, mask, queries, keys, values, name):
    heads, ctx, dim = keys.shape
    cols = (queries[0].shape[-1] // dim) * QB
    n = len(order)
    own = len([bits for bits in order if bits in EVEN])
    outs = []
    if own:
        outs.append(jax.ShapeDtypeStruct((own, dim + 8, mask.shape[0] * cols), jnp.float32))
    if n > own:
        outs.append(jax.ShapeDtypeStruct((n - own, dim + 16, mask.shape[0] * cols), jnp.bfloat16))
    return call(
        lambda *refs: cache_kernel(scale, order, *refs),
        name,
        outs,
        [IN_SMEM, IN_SMEM] + [IN_VMEM] * (len(queries) + 2),
        flops=(2 if own else 10) * n * queries[0].shape[-2] * heads * ctx * dim,
        nbytes=n * MIB,
        scratch=[
            pltpu.VMEM((mask.shape[0], n, cols, dim), jnp.bfloat16),
            pltpu.VMEM((mask.shape[0], n, dim, cols), jnp.float32),
            pltpu.SMEM((mask.size + 4,), jnp.int32),
            pltpu.VMEM((n, 2 * KB, cols), jnp.float32),
            pltpu.VMEM((mask.shape[0], n, 8, cols), jnp.float32),
        ],
    )(rank, mask, *queries, held(keys), held(values))


def merge_kernel(own_first, own_rest, got_first, got_rest, kept, *sent):
    dim = own_first.shape[1] - 8
    for i in range(4):
        own = own_first.at[0] if i == 0 else own_rest.at[i - 1]
        got = got_first.at[0] if i == 0 else got_rest.at[i - 1]
        mine, other = level_of(own[dim:, :]), level_of(got[dim:, :])
        top = jnp.maximum(mine, other)
        mine, other = jnp.exp2(mine - top), jnp.exp2(other - top)
        total = mine + other
        level = top + jnp.log2(total)
        mine, other = mine / total, other / total
        joined = own[:dim, :] * mine + got[:dim, :].astype(jnp.float32) * other
        target = kept if i == 0 else sent[i - 1]
        target[:dim, :] = joined.astype(target.dtype)
        target[dim:, :] = split_rows(level, target.shape[0] - dim).astype(target.dtype)


def output_kernel(
    rank,
    kept,
    got_a,
    got_b,
    got_c,
    summed,
    stats,
    weights,
    own,
    sent,
    rows,
    sorted_rows,
):
    dim = summed.shape[0]
    levels = [level_of(part[dim:, :]) for part in (kept, got_a, got_b, got_c)]
    top = stats[0:1, :]
    for level in levels:
        top = jnp.maximum(top, level)
    factor = jnp.exp2(stats[0:1, :] - top)
    total = stats[1:2, :] * factor
    joined = summed[...] * factor
    for part, level in zip((kept, got_a, got_b, got_c), levels):
        factor = jnp.exp2(level - top)
        total = total + factor
        joined = joined + part[:dim, :].astype(jnp.float32) * factor
    joined = joined * (1.0 / total)
    heads = rows.shape[1] // dim
    cols = heads * QB
    for q_block in range(rows.shape[0] // QB):
        turned = joined[:, q_block * cols : (q_block + 1) * cols].T
        for j in range(heads):
            rows[q_block * QB : (q_block + 1) * QB, j * dim : (j + 1) * dim] = turned[
                j * QB : (j + 1) * QB, :
            ]
    count = rows.shape[0] // 8
    for pair in range(4):
        chunk = [
            rows[pl.ds(pl.multiple_of((rank[0] ^ bits) * count, count), count), :]
            for bits in (EVEN + ODD)[2 * pair : 2 * pair + 2]
        ]
        sorted_rows[2 * count * pair : 2 * count * (pair + 1), :] = jnp.concatenate(
            chunk, axis=0
        ).astype(jnp.bfloat16)
    half = rows.shape[0] // 2
    step = 512
    for c in range(0, weights.shape[1], step):
        product = jnp.dot(
            sorted_rows[...], weights[:, c : c + step], preferred_element_type=jnp.float32
        )
        own[:, c : c + step] = product[:half]
        sent[:, c : c + step] = product[half:].astype(jnp.bfloat16)


def on_device_owned(
    tokens,
    norm_gain,
    w_query,
    key_projection,
    value_projection,
    w_out,
    key_cache,
    cached_value_rows,
    cache_mask,
    span_offset,
):
    n_seq = lax.axis_size("seq")
    rank = lax.axis_index("seq").astype(jnp.int32)[None]
    dim = key_cache.shape[3]
    count = tokens.shape[1]
    width = tokens.shape[2]
    tok = count * n_seq
    own_cols = w_query.shape[2]
    scale = dim ** (-0.5) * log2e
    mask = cache_mask[0]

    with jax.named_scope("cache_layout"):
        keys, values, layout_done = cache_by_head(rank, key_cache[0], cached_value_rows[0])
    with jax.named_scope("gather_tokens"):
        blocks = {0: tokens[0]}
        for bits in SAME_CORE:
            blocks[bits] = swapped(blocks[0], bits)
        same_core = joined_after([blocks[bits] for bits in EVEN], [layout_done], "join_tokens")
        other_core = swapped(same_core, 1)

    with jax.named_scope("tables"):
        positions = span_offset[0].astype(jnp.float32) + jnp.arange(tok, dtype=jnp.int32).astype(
            jnp.float32
        )
        freqs = rope_base ** (-2.0 * jnp.arange(dim // 2, dtype=jnp.float32) / dim)
        angles = positions[:, None] * freqs[None, :]
        cosine, sine = jnp.cos(angles), jnp.sin(angles)
        cosine = jnp.concatenate([cosine, cosine], axis=1)
        sine = jnp.concatenate([-sine, sine], axis=1)

    with jax.named_scope("queries"):
        query, normed = call(
            query_kernel,
            "queries",
            [
                jax.ShapeDtypeStruct((tok, own_cols), jnp.bfloat16),
                jax.ShapeDtypeStruct((tok, width), jnp.bfloat16),
            ],
            [IN_SMEM] + [IN_VMEM] * 6,
            flops=8 * tok * width * own_cols // 2,
            nbytes=16 * MIB,
            scratch=[pltpu.VMEM((tok, width), jnp.float32)],
        )(
            rank,
            same_core,
            other_core,
            norm_gain,
            cosine,
            sine,
            held(w_query[0]),
        )

    with jax.named_scope("gather_queries"):
        queries = {0: query}
        for bits in ODD:
            queries[bits] = swapped(query, bits)
    with jax.named_scope("new_tokens"):
        summed, stats = call(
            lambda *refs: new_kernel(scale, *refs),
            "new_tokens",
            [
                jax.ShapeDtypeStruct((dim, tok * own_cols // dim), jnp.float32),
                jax.ShapeDtypeStruct((8, tok * own_cols // dim), jnp.float32),
            ],
            [IN_VMEM] * 6,
            flops=16 * tok * width * dim,
            nbytes=5 * MIB,
        )(
            query,
            normed,
            held(key_projection[0]),
            held(value_projection[0]),
            cosine,
            sine,
        )

    with jax.named_scope("cache_near"):
        near_own, near_sent = cache_part(
            scale, (0, 1), rank, mask, [queries[0], queries[1]], keys, values, "cache_near"
        )
        near_got = swapped(near_sent, 1)
    with jax.named_scope("gather_queries"):
        far_odd = joined_after([queries[bits] for bits in ODD[1:]], [near_own], "join_queries")
        far_even = swapped(far_odd, 1)
    with jax.named_scope("cache_odd"):
        (odd,) = cache_part(scale, ODD[1:], rank, mask, [far_odd], keys, values, "cache_odd")
        odd_got = swapped(odd, 1)
    with jax.named_scope("cache_even"):
        (even,) = cache_part(scale, EVEN[1:], rank, mask, [far_even], keys, values, "cache_even")
    with jax.named_scope("merge_cores"):
        cols = even.shape[2]
        kept, *sent = call(
            merge_kernel,
            "merge_cores",
            [jax.ShapeDtypeStruct((dim + 8, cols), jnp.float32)]
            + [jax.ShapeDtypeStruct((dim + 16, cols), jnp.bfloat16)] * 3,
            [IN_VMEM] * 4,
            nbytes=2 * MIB,
        )(near_own, even, near_got, odd_got)
    with jax.named_scope("exchange_parts"):
        parts = [swapped(block, bits) for block, bits in zip(sent, SAME_CORE)]
    with jax.named_scope("project"):
        own, other = call(
            output_kernel,
            "project",
            [
                jax.ShapeDtypeStruct((tok // 2, width), jnp.float32),
                jax.ShapeDtypeStruct((tok // 2, width), jnp.bfloat16),
            ],
            [IN_SMEM] + [IN_VMEM] * 7,
            flops=8 * tok * width * own_cols // 2,
            nbytes=18 * MIB,
            scratch=[
                pltpu.VMEM((tok, own_cols), jnp.float32),
                pltpu.VMEM((tok, own_cols), jnp.bfloat16),
            ],
        )(rank, kept, *parts, summed, stats, held(w_out[0]))
    with jax.named_scope("reduce_cores"):
        pair = own + swapped(other, 1).astype(jnp.float32)
    with jax.named_scope("reduce_on_next_section"):
        total = 0.0
        for i, bits in enumerate(EVEN):
            block = pair[i * count : (i + 1) * count]
            if bits == 0:
                block = tokens[0].astype(jnp.float32) + block
            total = total + onward(block.astype(jnp.bfloat16), bits).astype(jnp.float32)
        handed = total.astype(jnp.bfloat16)
    return handed[None]


def on_device(*arrays):
    tokens, w_query, key_projection, key_cache = arrays[0], arrays[2], arrays[3], arrays[6]
    head_dim = key_cache.shape[3]
    kv_heads = key_cache.shape[2]
    n_seq = lax.axis_size("seq")
    tok_all = tokens.shape[1] * n_seq
    if (
        n_seq == kv_heads == 8
        and key_projection.shape[2] == head_dim == 128
        and tokens.shape[1] == 8
        and tok_all == 2 * QB
    ):
        return on_device_owned(*arrays)
    return on_device_any(*arrays)


def solution(mesh):
    placed = (
        P("section", "seq", None),
        P("section", None),
        P("section", None, "seq"),
        P("section", None, "seq"),
        P("section", None, "seq"),
        P("section", "seq", None),
        P("section", "seq", None, None),
        P("section", "seq", None, None),
        P("section", None, "seq"),
        P("section"),
    )
    return jax.shard_map(
        on_device, mesh=mesh, in_specs=placed, out_specs=P("section", "seq", None), check_vma=False
    )
```

```python
import functools

import jax
import jax.numpy as jnp
from jax import lax
from jax.experimental import pallas as pl
from jax.experimental.pallas import tpu as pltpu
from jax.sharding import PartitionSpec as P

QB = 32
KB = 128


rope_base = 500000.0
neg_fill = -1e30
norm_eps = 1e-05


def passed_along(block, axis, distance):
    devices = range(lax.axis_size(axis))
    route = [((i - distance) % len(devices), i) for i in devices]
    return lax.ppermute(block, axis, route)


def apply_rotation(values, token_positions):
    half = values.shape[-1] // 2
    freqs = rope_base ** (-2.0 * jnp.arange(half, dtype=jnp.float32) / values.shape[-1])
    angles = token_positions[:, None] * freqs[None, :]
    cosine = jnp.cos(angles)[:, None, :]
    sine = jnp.sin(angles)[:, None, :]
    first = values[..., :half]
    second = values[..., half:]
    return jnp.concatenate(
        [first * cosine - second * sine, second * cosine + first * sine], axis=-1
    )


def on_device_any(
    tokens,
    norm_gain,
    w_query,
    key_projection,
    value_projection,
    w_out,
    key_cache,
    cached_value_rows,
    cache_mask,
    span_offset,
):
    n_seq = lax.axis_size("seq")
    rank = lax.axis_index("seq")
    head_dim = key_cache.shape[3]
    kv_heads = key_cache.shape[2]
    own_heads = w_query.shape[2] // head_dim
    all_heads = own_heads * n_seq
    group = all_heads // kv_heads
    tok_local = tokens.shape[1]
    tok_all = tok_local * n_seq
    ctx_local = key_cache.shape[1]
    scale = head_dim ** (-0.5)
    query_cols = own_heads * head_dim
    key_cols = key_projection.shape[2]
    offset = span_offset[0].astype(jnp.float32)
    resid = tokens[0].astype(jnp.float32)
    mean_square = jnp.mean(resid * resid, axis=-1, keepdims=True)
    input_normalized = (
        resid * lax.rsqrt(mean_square + norm_eps) * norm_gain[0].astype(jnp.float32)
    ).astype(jnp.bfloat16)
    piece = lax.all_gather(input_normalized, "seq", axis=0, tiled=True)
    rows = piece.shape[0]
    token_positions = offset + jnp.arange(rows, dtype=jnp.int32).astype(jnp.float32)
    query = jnp.dot(piece, w_query[0], preferred_element_type=jnp.float32)
    query = apply_rotation(query.reshape(rows, own_heads, head_dim), token_positions).reshape(
        rows, query_cols
    )
    key_unrotated = jnp.dot(piece, key_projection[0], preferred_element_type=jnp.float32)
    value_raw = jnp.dot(piece, value_projection[0], preferred_element_type=jnp.float32)
    fresh = jnp.concatenate([query, key_unrotated, value_raw], axis=1).astype(jnp.bfloat16)
    own_query = fresh[:, :query_cols]
    query_all, key_all, value_all = (
        lax.all_gather(own_query, "seq", axis=1, tiled=True),
        lax.all_gather(fresh[:, query_cols : query_cols + key_cols], "seq", axis=1, tiled=True),
        lax.all_gather(fresh[:, query_cols + key_cols :], "seq", axis=1, tiled=True),
    )
    positions_all = offset + jnp.arange(tok_all, dtype=jnp.int32).astype(jnp.float32)
    key_rot = apply_rotation(
        key_all.astype(jnp.float32).reshape(tok_all, kv_heads, head_dim), positions_all
    ).astype(jnp.bfloat16)
    value_heads = value_all.reshape(tok_all, kv_heads, head_dim)
    query_grouped = query_all.reshape(tok_all, kv_heads, group, head_dim)
    block = min(512, ctx_local)
    per_block = block // KB
    q_blocks = tok_all // QB

    def cache_step(index, carry):
        top, total, summed = carry
        keys = lax.dynamic_slice_in_dim(key_cache[0], index * block, block, 0)
        values = lax.dynamic_slice_in_dim(cached_value_rows[0], index * block, block, 0)
        visible = lax.dynamic_slice_in_dim(cache_mask[0], index * per_block, per_block, 1) > 0
        scores = (
            jnp.einsum("tgjd,cgd->tgjc", query_grouped, keys, preferred_element_type=jnp.float32)
            * scale
        )
        shaped = scores.reshape(q_blocks, QB, kv_heads, group, per_block, KB)
        allowed = visible[:, None, None, None, :, None]
        shaped = jnp.where(allowed, shaped, neg_fill)
        block_top = jnp.max(shaped, axis=(4, 5)).reshape(tok_all, kv_heads, group)
        new_top = jnp.maximum(top, block_top)
        lifted = new_top.reshape(q_blocks, QB, kv_heads, group, 1, 1)
        weights = jnp.where(allowed, jnp.exp(shaped - lifted), 0.0).reshape(
            tok_all, kv_heads, group, block
        )
        factor = jnp.exp(top - new_top)
        total = total * factor + jnp.sum(weights, axis=-1)
        summed = summed * factor[..., None] + jnp.einsum(
            "tgjc,cgd->tgjd",
            weights.astype(jnp.bfloat16),
            values,
            preferred_element_type=jnp.float32,
        )
        return (new_top, total, summed)

    start_top = jnp.full((tok_all, kv_heads, group), neg_fill, jnp.float32)
    start_total = jnp.zeros((tok_all, kv_heads, group), jnp.float32)
    start_sum = jnp.zeros((tok_all, kv_heads, group, head_dim), jnp.float32)
    top, total, summed = lax.fori_loop(
        0, ctx_local // block, cache_step, (start_top, start_total, start_sum)
    )
    top = top.reshape(tok_all, all_heads)
    total = total.reshape(tok_all, all_heads)
    summed = summed.reshape(tok_all, all_heads, head_dim)
    got_sum, got_top, got_total = (
        lax.all_to_all(summed[None], "seq", split_axis=2, concat_axis=0, tiled=True),
        lax.all_to_all(top[None], "seq", split_axis=2, concat_axis=0, tiled=True),
        lax.all_to_all(total[None], "seq", split_axis=2, concat_axis=0, tiled=True),
    )
    cache_top = jnp.max(got_top, axis=0)
    factor = jnp.exp(got_top - cache_top[None])
    cache_total = jnp.sum(got_total * factor, axis=0)
    cache_sum = jnp.sum(got_sum * factor[..., None], axis=0)
    kv_index = (rank * own_heads + jnp.arange(own_heads, dtype=jnp.int32)) // group
    own_keys = jnp.take(key_rot, kv_index, axis=1)
    own_values = jnp.take(value_heads, kv_index, axis=1)
    own_q = own_query.reshape(tok_all, own_heads, head_dim)
    self_scores = (
        jnp.einsum("thd,shd->ths", own_q, own_keys, preferred_element_type=jnp.float32) * scale
    )
    row_ids = jnp.arange(tok_all, dtype=jnp.int32)
    causal = (row_ids[None, :] <= row_ids[:, None])[:, None, :]
    self_scores = jnp.where(causal, self_scores, neg_fill)
    top_all = jnp.maximum(cache_top, jnp.max(self_scores, axis=-1))
    cache_factor = jnp.exp(cache_top - top_all)
    self_weights = jnp.where(causal, jnp.exp(self_scores - top_all[..., None]), 0.0)
    total_all = cache_total * cache_factor + jnp.sum(self_weights, axis=-1)
    sum_all = cache_sum * cache_factor[..., None] + jnp.einsum(
        "ths,shd->thd",
        self_weights.astype(jnp.bfloat16),
        own_values,
        preferred_element_type=jnp.float32,
    )
    attention = (sum_all / total_all[..., None]).reshape(tok_all, query_cols).astype(jnp.bfloat16)
    projected = lax.psum_scatter(
        jnp.dot(attention, w_out[0], preferred_element_type=jnp.float32).astype(jnp.bfloat16),
        "seq",
        scatter_dimension=0,
        tiled=True,
    ).astype(jnp.float32)
    layer_out = (resid + projected).astype(jnp.bfloat16)
    handed = passed_along(layer_out, "section", 1)
    return handed[None]


MIB = 1 << 20
log2e = 1.4426950408889634
IN_VMEM = pl.BlockSpec(memory_space=pltpu.VMEM)
IN_SMEM = pl.BlockSpec(memory_space=pltpu.SMEM)
SAME_CORE = (2, 4, 6)
EVEN = (0, 2, 4, 6)
ODD = (1, 3, 5, 7)


def swapped(block, bits):
    n = lax.axis_size("seq")
    return lax.ppermute(block, "seq", [(i, i ^ bits) for i in range(n)])


def onward(block, bits):
    sections, n = lax.axis_size("section"), lax.axis_size("seq")
    route = [
        (s * n + i, (s + 1) % sections * n + (i ^ bits)) for s in range(sections) for i in range(n)
    ]
    return lax.ppermute(block, ("section", "seq"), route)


def call(kernel, name, out_shape, in_specs, flops=0, nbytes=0, scratch=(), vmem=6, **grid):
    out_specs = grid.pop("out_specs", jax.tree.map(lambda _: IN_VMEM, out_shape))
    return pl.pallas_call(
        kernel,
        out_shape=out_shape,
        in_specs=in_specs,
        out_specs=out_specs,
        scratch_shapes=list(scratch),
        name=name,
        cost_estimate=pl.CostEstimate(flops=flops, bytes_accessed=nbytes, transcendentals=0),
        compiler_params=pltpu.CompilerParams(vmem_limit_bytes=vmem * MIB),
        **grid,
    )


def held(array):
    return pltpu.with_memory_space_constraint(array, pltpu.VMEM)


def join_kernel(count, *refs):
    for i in range(count):
        refs[-1][i] = refs[i][...]


def joined_after(blocks, done, name):
    count = len(blocks)
    return call(
        lambda *refs: join_kernel(count, *refs),
        name,
        jax.ShapeDtypeStruct((count, *blocks[0].shape), blocks[0].dtype),
        [IN_VMEM] * count + [pl.BlockSpec(memory_space=pl.ANY)] * len(done),
        nbytes=MIB,
        vmem=2,
    )(*blocks, *done)


def rotated(heads, cosine, sine):
    half = heads.shape[1] // 2
    return heads * cosine + pltpu.roll(heads, half, 1) * sine


def query_kernel(rank, *refs):
    same_core, other_core, gain, cosine, sine, weights, query, normed, rows = refs
    width = rows.shape[1]
    count = same_core.shape[1]
    blocks = [part.at[i] for i in range(4) for part in (same_core, other_core)]
    step = 1024
    for bits in range(8):
        at = pl.multiple_of((rank[0] ^ bits) * count, count)
        rows[pl.ds(at, count), :] = blocks[bits][...].astype(jnp.float32)
    squares = jnp.zeros((rows.shape[0], 128), jnp.float32)
    for c in range(0, width, 128):
        part = rows[:, c : c + 128]
        squares = squares + part * part
    mean_square = jnp.sum(squares, axis=-1, keepdims=True) / width
    factor = lax.rsqrt(mean_square + norm_eps)
    for c in range(0, width, step):
        normed[:, c : c + step] = (
            rows[:, c : c + step] * factor * gain[:, c : c + step].astype(jnp.float32)
        ).astype(jnp.bfloat16)
    dim = cosine.shape[1]
    for c in range(0, weights.shape[1], 2 * dim):
        raw = jnp.dot(
            normed[...], weights[:, c : c + 2 * dim], preferred_element_type=jnp.float32
        )
        for d in range(0, 2 * dim, dim):
            query[:, c + d : c + d + dim] = rotated(
                raw[:, d : d + dim], cosine[...], sine[...]
            ).astype(jnp.bfloat16)


def query_rows(query, q_block, heads, dim):
    rows = slice(q_block * QB, (q_block + 1) * QB)
    return jnp.concatenate([query[rows, j * dim : (j + 1) * dim] for j in range(heads)], axis=0)


def matmul_nt(a, b):
    return lax.dot_general(a, b, (((1,), (1,)), ((), ())), preferred_element_type=jnp.float32)


def by_head_kernel(rank, keys, values, keys_out, values_out, done, keys_in, values_in, sems):
    blocks = sems.shape[1]
    block = keys.shape[0] // blocks

    def copies(i):
        at = pl.ds(pl.multiple_of(i * block, block), block)
        return [
            pltpu.make_async_copy(source.at[at], target.at[at], sems.at[which, i])
            for which, (source, target) in enumerate([(keys, keys_in), (values, values_in)])
        ]

    @pl.loop(0, blocks)
    def _(i):
        for copy in copies(i):
            copy.start()

    done[...] = jnp.zeros_like(done)

    @pl.loop(0, blocks)
    def _(i):
        at = pl.ds(pl.multiple_of(i * block, block), block)
        for copy in copies(i):
            copy.wait()
        keys_out[:, at, :] = jnp.swapaxes(keys_in[at], 0, 1)
        turned = jnp.swapaxes(values_in[at], 0, 1)
        for g in range(turned.shape[0]):
            values_out[g, :, at] = turned[g].T


def cache_by_head(rank, keys, values):
    ctx, heads, dim = keys.shape
    blocks = 8
    in_hbm = pl.BlockSpec(memory_space=pltpu.HBM)
    return call(
        by_head_kernel,
        "cache_by_head",
        [
            jax.ShapeDtypeStruct((heads, ctx, dim), jnp.bfloat16),
            jax.ShapeDtypeStruct((heads, dim, ctx), jnp.bfloat16),
            jax.ShapeDtypeStruct((8, 128), jnp.float32),
        ],
        [IN_SMEM, in_hbm, in_hbm],
        flops=10**10,
        nbytes=ctx * heads * dim * 2,
        scratch=[
            pltpu.VMEM(keys.shape, jnp.bfloat16),
            pltpu.VMEM(values.shape, jnp.bfloat16),
            pltpu.SemaphoreType.DMA((2, blocks)),
        ],
        vmem=14,
    )(
        rank,
        pltpu.with_memory_space_constraint(keys, pltpu.HBM),
        pltpu.with_memory_space_constraint(values, pltpu.HBM),
    )


def new_kernel(
    scale,
    query,
    normed,
    w_key,
    w_value,
    cosine,
    sine,
    summed,
    stats,
):
    tok, dim = cosine.shape
    heads = query.shape[1] // dim
    raw = jnp.dot(normed[...], w_key[...], preferred_element_type=jnp.float32)
    raw = raw.astype(jnp.bfloat16).astype(jnp.float32)
    keys = rotated(raw, cosine[...], sine[...]).astype(jnp.bfloat16)
    values = jnp.dot(normed[...], w_value[...], preferred_element_type=jnp.float32)
    values = values.astype(jnp.bfloat16).astype(jnp.float32).T.astype(jnp.bfloat16)
    cols = heads * QB
    for q_block in range(tok // QB):
        scores = matmul_nt(keys, query_rows(query, q_block, heads, dim)) * scale
        u = lax.broadcasted_iota(jnp.int32, (tok, cols), 0)
        t = lax.broadcasted_iota(jnp.int32, (tok, cols), 1) % QB + q_block * QB
        allowed = u <= t
        scores = jnp.where(allowed, scores, neg_fill)
        top = jnp.max(scores, axis=0, keepdims=True)
        weights = jnp.where(allowed, jnp.exp2(scores - top), 0.0)
        at = slice(q_block * cols, (q_block + 1) * cols)
        stats[0:1, at] = top
        stats[1:2, at] = jnp.sum(weights, axis=0, keepdims=True)
        summed[:, at] = jnp.dot(
            values, weights.astype(jnp.bfloat16), preferred_element_type=jnp.float32
        )


def split_rows(level, rows):
    high = level.astype(jnp.bfloat16).astype(jnp.float32)
    rest = level - high
    middle = rest.astype(jnp.bfloat16).astype(jnp.float32)
    low = rest - middle
    row = lax.broadcasted_iota(jnp.int32, (rows, level.shape[1]), 0)
    return jnp.where(row == 0, high, jnp.where(row == 1, middle, jnp.where(row == 2, low, 0.0)))


def level_of(tail):
    tail = tail.astype(jnp.float32)
    return tail[0:1] + tail[1:2] + tail[2:3]


def cache_kernel(scale, order, rank, mask, *refs):
    n = len(order)
    given = 1 if len(refs[0].shape) == 3 else n
    queries, (keys, values), outs = refs[:given], refs[given : given + 2], refs[given + 2 : -5]
    if given < n:
        queries = [queries[0].at[i] for i in range(n)]
    q_rows, summed, visible, scores, levels = refs[-5:]
    dim = keys.shape[2]
    heads = queries[0].shape[1] // dim
    cols = heads * QB
    groups = [rank[0] ^ bits for bits in order]
    own = [bits for bits in order if bits in EVEN]
    blocks = mask.shape[0]
    place = jnp.int32(0)
    ends, singles = [], []
    for q_block in range(blocks):
        for b in range(mask.shape[1]):
            visible[place] = b
            place = place + (mask[q_block, b] > 0).astype(jnp.int32)
        visible[place] = 0
        odd = place % 2
        place = place + odd
        ends.append(place // 2)
        singles.append(jnp.where(odd == 1, place // 2 - 1, -1))
        for i in range(n):
            q_rows[q_block, i] = query_rows(queries[i], q_block, heads, dim)
            summed[q_block, i] = jnp.zeros((dim, cols), jnp.float32)
            levels[q_block, i, 0:1] = jnp.full((1, cols), neg_fill, jnp.float32)
            levels[q_block, i, 1:2] = jnp.zeros((1, cols), jnp.float32)
    for e in range(2):
        visible[place + e] = 0

    def q_block_of(pair):
        return sum((pair >= end).astype(jnp.int32) for end in ends[:-1])

    def places(pair):
        return [pl.multiple_of(visible[2 * pair + e] * KB, KB) for e in range(2)]

    def score(pair):
        at = places(pair)
        q_block = q_block_of(pair)
        single = functools.reduce(jnp.logical_or, [pair == one for one in singles])
        hidden = jnp.where(single, jnp.float32(neg_fill), jnp.float32(0.0))
        products = [
            matmul_nt(
                jnp.concatenate([keys[g, pl.ds(a, KB), :] for a in at], axis=0),
                q_rows[q_block, i],
            )
            for i, g in enumerate(groups)
        ]
        tops = []
        for i in range(n):
            first = products[i][:KB] * scale
            second = products[i][KB:] * scale + hidden
            scores[i, :KB] = first
            scores[i, KB:] = second
            tops.append(jnp.max(jnp.maximum(first, second), axis=0, keepdims=True))
        return tops

    def step(pair, tops):
        q_block = q_block_of(pair)
        scaled = []
        for i in range(n):
            top, total = levels[q_block, i, 0:1], levels[q_block, i, 1:2]
            new_top = jnp.maximum(top, tops[i])
            weights = jnp.exp2(scores[i] - new_top)
            factor = jnp.exp2(top - new_top)
            levels[q_block, i, 0:1] = new_top
            levels[q_block, i, 1:2] = total * factor + jnp.sum(weights, axis=0, keepdims=True)
            scaled.append((factor, weights.astype(jnp.bfloat16)))
        at = places(pair)
        products = [
            jnp.dot(
                jnp.concatenate([values[g, :, pl.ds(a, KB)] for a in at], axis=1),
                scaled[i][1],
                preferred_element_type=jnp.float32,
            )
            for i, g in enumerate(groups)
        ]
        tops = score(pair + 1)
        for i in range(n):
            summed[q_block, i] = summed[q_block, i] * scaled[i][0] + products[i]
        return tuple(tops)

    lax.fori_loop(0, ends[-1], step, tuple(score(jnp.int32(0))))
    for q_block in range(blocks):
        at = slice(q_block * cols, (q_block + 1) * cols)
        for i, bits in enumerate(order):
            top, total = levels[q_block, i, 0:1], levels[q_block, i, 1:2]
            seen = total > 0.0
            safe = jnp.where(seen, total, 1.0)
            level = jnp.where(seen, top + jnp.log2(safe), neg_fill)
            if bits in EVEN:
                out, place = outs[0], own.index(bits)
            else:
                out, place = outs[-1], i - len(own)
            out[place, 0:dim, at] = (summed[q_block, i] * (1.0 / safe)).astype(out.dtype)
            out[place, dim:, at] = split_rows(level, out.shape[1] - dim).astype(out.dtype)


def cache_part(scale, order, rank, mask, queries, keys, values, name):
    heads, ctx, dim = keys.shape
    cols = (queries[0].shape[-1] // dim) * QB
    n = len(order)
    own = len([bits for bits in order if bits in EVEN])
    outs = []
    if own:
        outs.append(jax.ShapeDtypeStruct((own, dim + 8, mask.shape[0] * cols), jnp.float32))
    if n > own:
        outs.append(jax.ShapeDtypeStruct((n - own, dim + 16, mask.shape[0] * cols), jnp.bfloat16))
    return call(
        lambda *refs: cache_kernel(scale, order, *refs),
        name,
        outs,
        [IN_SMEM, IN_SMEM] + [IN_VMEM] * (len(queries) + 2),
        flops=(2 if own else 10) * n * queries[0].shape[-2] * heads * ctx * dim,
        nbytes=n * MIB,
        scratch=[
            pltpu.VMEM((mask.shape[0], n, cols, dim), jnp.bfloat16),
            pltpu.VMEM((mask.shape[0], n, dim, cols), jnp.float32),
            pltpu.SMEM((mask.size + 4,), jnp.int32),
            pltpu.VMEM((n, 2 * KB, cols), jnp.float32),
            pltpu.VMEM((mask.shape[0], n, 8, cols), jnp.float32),
        ],
    )(rank, mask, *queries, held(keys), held(values))


def merge_kernel(own_first, own_rest, got_first, got_rest, kept, *sent):
    dim = own_first.shape[1] - 8
    for i in range(4):
        own = own_first.at[0] if i == 0 else own_rest.at[i - 1]
        got = got_first.at[0] if i == 0 else got_rest.at[i - 1]
        mine, other = level_of(own[dim:, :]), level_of(got[dim:, :])
        top = jnp.maximum(mine, other)
        mine, other = jnp.exp2(mine - top), jnp.exp2(other - top)
        total = mine + other
        level = top + jnp.log2(total)
        mine, other = mine / total, other / total
        joined = own[:dim, :] * mine + got[:dim, :].astype(jnp.float32) * other
        target = kept if i == 0 else sent[i - 1]
        target[:dim, :] = joined.astype(target.dtype)
        target[dim:, :] = split_rows(level, target.shape[0] - dim).astype(target.dtype)


def output_kernel(
    rank,
    kept,
    got_a,
    got_b,
    got_c,
    summed,
    stats,
    weights,
    own,
    sent,
    rows,
    sorted_rows,
):
    dim = summed.shape[0]
    levels = [level_of(part[dim:, :]) for part in (kept, got_a, got_b, got_c)]
    top = stats[0:1, :]
    for level in levels:
        top = jnp.maximum(top, level)
    factor = jnp.exp2(stats[0:1, :] - top)
    total = stats[1:2, :] * factor
    joined = summed[...] * factor
    for part, level in zip((kept, got_a, got_b, got_c), levels):
        factor = jnp.exp2(level - top)
        total = total + factor
        joined = joined + part[:dim, :].astype(jnp.float32) * factor
    joined = joined * (1.0 / total)
    heads = rows.shape[1] // dim
    cols = heads * QB
    for q_block in range(rows.shape[0] // QB):
        turned = joined[:, q_block * cols : (q_block + 1) * cols].T
        for j in range(heads):
            rows[q_block * QB : (q_block + 1) * QB, j * dim : (j + 1) * dim] = turned[
                j * QB : (j + 1) * QB, :
            ]
    count = rows.shape[0] // 8
    for pair in range(4):
        chunk = [
            rows[pl.ds(pl.multiple_of((rank[0] ^ bits) * count, count), count), :]
            for bits in (EVEN + ODD)[2 * pair : 2 * pair + 2]
        ]
        sorted_rows[2 * count * pair : 2 * count * (pair + 1), :] = jnp.concatenate(
            chunk, axis=0
        ).astype(jnp.bfloat16)
    half = rows.shape[0] // 2
    step = 512
    for c in range(0, weights.shape[1], step):
        product = jnp.dot(
            sorted_rows[...], weights[:, c : c + step], preferred_element_type=jnp.float32
        )
        own[:, c : c + step] = product[:half]
        sent[:, c : c + step] = product[half:].astype(jnp.bfloat16)


def pair_kernel(own, got, resid, *outs):
    count = resid.shape[0]
    for i, out in enumerate(outs):
        rows = slice(i * count, (i + 1) * count)
        block = own[rows] + got[...].astype(jnp.float32)[rows]
        if i == 0:
            block = resid[...].astype(jnp.float32) + block
        out[...] = block.astype(out.dtype)


def add_kernel(block, across, out):
    out[...] = (block[...] + across[...].astype(jnp.float32)).astype(out.dtype)


def on_device_owned(
    tokens,
    norm_gain,
    w_query,
    key_projection,
    value_projection,
    w_out,
    key_cache,
    cached_value_rows,
    cache_mask,
    span_offset,
):
    n_seq = lax.axis_size("seq")
    rank = lax.axis_index("seq").astype(jnp.int32)[None]
    dim = key_cache.shape[3]
    count = tokens.shape[1]
    width = tokens.shape[2]
    tok = count * n_seq
    own_cols = w_query.shape[2]
    scale = dim ** (-0.5) * log2e
    mask = cache_mask[0]

    with jax.named_scope("cache_layout"):
        keys, values, layout_done = cache_by_head(rank, key_cache[0], cached_value_rows[0])
    with jax.named_scope("gather_tokens"):
        blocks = {0: tokens[0]}
        for bits in SAME_CORE:
            blocks[bits] = swapped(blocks[0], bits)
        same_core = joined_after([blocks[bits] for bits in EVEN], [layout_done], "join_tokens")
        other_core = swapped(same_core, 1)

    with jax.named_scope("tables"):
        positions = span_offset[0].astype(jnp.float32) + jnp.arange(tok, dtype=jnp.int32).astype(
            jnp.float32
        )
        freqs = rope_base ** (-2.0 * jnp.arange(dim // 2, dtype=jnp.float32) / dim)
        angles = positions[:, None] * freqs[None, :]
        cosine, sine = jnp.cos(angles), jnp.sin(angles)
        cosine = jnp.concatenate([cosine, cosine], axis=1)
        sine = jnp.concatenate([-sine, sine], axis=1)

    with jax.named_scope("queries"):
        query, normed = call(
            query_kernel,
            "queries",
            [
                jax.ShapeDtypeStruct((tok, own_cols), jnp.bfloat16),
                jax.ShapeDtypeStruct((tok, width), jnp.bfloat16),
            ],
            [IN_SMEM] + [IN_VMEM] * 6,
            flops=8 * tok * width * own_cols // 2,
            nbytes=16 * MIB,
            scratch=[pltpu.VMEM((tok, width), jnp.float32)],
        )(
            rank,
            same_core,
            other_core,
            norm_gain,
            cosine,
            sine,
            held(w_query[0]),
        )

    with jax.named_scope("gather_queries"):
        queries = {0: query}
        for bits in ODD:
            queries[bits] = swapped(query, bits)
    with jax.named_scope("new_tokens"):
        summed, stats = call(
            lambda *refs: new_kernel(scale, *refs),
            "new_tokens",
            [
                jax.ShapeDtypeStruct((dim, tok * own_cols // dim), jnp.float32),
                jax.ShapeDtypeStruct((8, tok * own_cols // dim), jnp.float32),
            ],
            [IN_VMEM] * 6,
            flops=16 * tok * width * dim,
            nbytes=5 * MIB,
        )(
            query,
            normed,
            held(key_projection[0]),
            held(value_projection[0]),
            cosine,
            sine,
        )

    with jax.named_scope("cache_near"):
        near_own, near_sent = cache_part(
            scale, (0, 1), rank, mask, [queries[0], queries[1]], keys, values, "cache_near"
        )
        near_got = swapped(near_sent, 1)
    with jax.named_scope("gather_queries"):
        far_odd = joined_after([queries[bits] for bits in ODD[1:]], [near_own], "join_queries")
        far_even = swapped(far_odd, 1)
    with jax.named_scope("cache_odd"):
        (odd,) = cache_part(scale, ODD[1:], rank, mask, [far_odd], keys, values, "cache_odd")
        odd_got = swapped(odd, 1)
    with jax.named_scope("cache_even"):
        (even,) = cache_part(scale, EVEN[1:], rank, mask, [far_even], keys, values, "cache_even")
    with jax.named_scope("merge_cores"):
        cols = even.shape[2]
        kept, *sent = call(
            merge_kernel,
            "merge_cores",
            [jax.ShapeDtypeStruct((dim + 8, cols), jnp.float32)]
            + [jax.ShapeDtypeStruct((dim + 16, cols), jnp.bfloat16)] * 3,
            [IN_VMEM] * 4,
            nbytes=2 * MIB,
        )(near_own, even, near_got, odd_got)
    with jax.named_scope("exchange_parts"):
        parts = [swapped(block, bits) for block, bits in zip(sent, SAME_CORE)]
    with jax.named_scope("project"):
        own, other = call(
            output_kernel,
            "project",
            [
                jax.ShapeDtypeStruct((tok // 2, width), jnp.float32),
                jax.ShapeDtypeStruct((tok // 2, width), jnp.bfloat16),
            ],
            [IN_SMEM] + [IN_VMEM] * 7,
            flops=8 * tok * width * own_cols // 2,
            nbytes=18 * MIB,
            scratch=[
                pltpu.VMEM((tok, own_cols), jnp.float32),
                pltpu.VMEM((tok, own_cols), jnp.bfloat16),
            ],
        )(rank, kept, *parts, summed, stats, held(w_out[0]))
    with jax.named_scope("reduce_cores"):
        row = jax.ShapeDtypeStruct((count, width), jnp.bfloat16)
        row_f32 = jax.ShapeDtypeStruct((count, width), jnp.float32)
        at_own, at_x, at_y, to_x = call(
            pair_kernel, "reduce_cores", [row, row, row_f32, row], [IN_VMEM] * 3, nbytes=2 * MIB
        )(own, swapped(other, 1), tokens[0])
    with jax.named_scope("reduce_on_next_section"):
        across = swapped(to_x, EVEN[1])
        from_own, from_x = onward(at_own, EVEN[0]), onward(at_x, EVEN[1])
        at_y = call(add_kernel, "add_across", row, [IN_VMEM] * 2)(at_y, across)
        total = from_own.astype(jnp.float32) + from_x.astype(jnp.float32)
        total = total + onward(at_y, EVEN[2]).astype(jnp.float32)
        handed = total.astype(jnp.bfloat16)
    return handed[None]


def on_device(*arrays):
    tokens, w_query, key_projection, key_cache = arrays[0], arrays[2], arrays[3], arrays[6]
    head_dim = key_cache.shape[3]
    kv_heads = key_cache.shape[2]
    n_seq = lax.axis_size("seq")
    tok_all = tokens.shape[1] * n_seq
    if (
        n_seq == kv_heads == 8
        and key_projection.shape[2] == head_dim == 128
        and tokens.shape[1] == 8
        and tok_all == 2 * QB
    ):
        return on_device_owned(*arrays)
    return on_device_any(*arrays)


def solution(mesh):
    placed = (
        P("section", "seq", None),
        P("section", None),
        P("section", None, "seq"),
        P("section", None, "seq"),
        P("section", None, "seq"),
        P("section", "seq", None),
        P("section", "seq", None, None),
        P("section", "seq", None, None),
        P("section", None, "seq"),
        P("section"),
    )
    return jax.shard_map(
        on_device, mesh=mesh, in_specs=placed, out_specs=P("section", "seq", None), check_vma=False
    )
```

```python
import functools

import jax
import jax.numpy as jnp
from jax import lax
from jax.experimental import pallas as pl
from jax.experimental.pallas import tpu as pltpu
from jax.sharding import PartitionSpec as P

QB = 32
KB = 128


rope_base = 500000.0
neg_fill = -1e30
norm_eps = 1e-05


def passed_along(block, axis, distance):
    devices = range(lax.axis_size(axis))
    route = [((i - distance) % len(devices), i) for i in devices]
    return lax.ppermute(block, axis, route)


def apply_rotation(values, token_positions):
    half = values.shape[-1] // 2
    freqs = rope_base ** (-2.0 * jnp.arange(half, dtype=jnp.float32) / values.shape[-1])
    angles = token_positions[:, None] * freqs[None, :]
    cosine = jnp.cos(angles)[:, None, :]
    sine = jnp.sin(angles)[:, None, :]
    first = values[..., :half]
    second = values[..., half:]
    return jnp.concatenate(
        [first * cosine - second * sine, second * cosine + first * sine], axis=-1
    )


def on_device_any(
    tokens,
    norm_gain,
    w_query,
    key_projection,
    value_projection,
    w_out,
    key_cache,
    cached_value_rows,
    cache_mask,
    span_offset,
):
    n_seq = lax.axis_size("seq")
    rank = lax.axis_index("seq")
    head_dim = key_cache.shape[3]
    kv_heads = key_cache.shape[2]
    own_heads = w_query.shape[2] // head_dim
    all_heads = own_heads * n_seq
    group = all_heads // kv_heads
    tok_local = tokens.shape[1]
    tok_all = tok_local * n_seq
    ctx_local = key_cache.shape[1]
    scale = head_dim ** (-0.5)
    query_cols = own_heads * head_dim
    key_cols = key_projection.shape[2]
    offset = span_offset[0].astype(jnp.float32)
    resid = tokens[0].astype(jnp.float32)
    mean_square = jnp.mean(resid * resid, axis=-1, keepdims=True)
    input_normalized = (
        resid * lax.rsqrt(mean_square + norm_eps) * norm_gain[0].astype(jnp.float32)
    ).astype(jnp.bfloat16)
    piece = lax.all_gather(input_normalized, "seq", axis=0, tiled=True)
    rows = piece.shape[0]
    token_positions = offset + jnp.arange(rows, dtype=jnp.int32).astype(jnp.float32)
    query = jnp.dot(piece, w_query[0], preferred_element_type=jnp.float32)
    query = apply_rotation(query.reshape(rows, own_heads, head_dim), token_positions).reshape(
        rows, query_cols
    )
    key_unrotated = jnp.dot(piece, key_projection[0], preferred_element_type=jnp.float32)
    value_raw = jnp.dot(piece, value_projection[0], preferred_element_type=jnp.float32)
    fresh = jnp.concatenate([query, key_unrotated, value_raw], axis=1).astype(jnp.bfloat16)
    own_query = fresh[:, :query_cols]
    query_all, key_all, value_all = (
        lax.all_gather(own_query, "seq", axis=1, tiled=True),
        lax.all_gather(fresh[:, query_cols : query_cols + key_cols], "seq", axis=1, tiled=True),
        lax.all_gather(fresh[:, query_cols + key_cols :], "seq", axis=1, tiled=True),
    )
    positions_all = offset + jnp.arange(tok_all, dtype=jnp.int32).astype(jnp.float32)
    key_rot = apply_rotation(
        key_all.astype(jnp.float32).reshape(tok_all, kv_heads, head_dim), positions_all
    ).astype(jnp.bfloat16)
    value_heads = value_all.reshape(tok_all, kv_heads, head_dim)
    query_grouped = query_all.reshape(tok_all, kv_heads, group, head_dim)
    block = min(512, ctx_local)
    per_block = block // KB
    q_blocks = tok_all // QB

    def cache_step(index, carry):
        top, total, summed = carry
        keys = lax.dynamic_slice_in_dim(key_cache[0], index * block, block, 0)
        values = lax.dynamic_slice_in_dim(cached_value_rows[0], index * block, block, 0)
        visible = lax.dynamic_slice_in_dim(cache_mask[0], index * per_block, per_block, 1) > 0
        scores = (
            jnp.einsum("tgjd,cgd->tgjc", query_grouped, keys, preferred_element_type=jnp.float32)
            * scale
        )
        shaped = scores.reshape(q_blocks, QB, kv_heads, group, per_block, KB)
        allowed = visible[:, None, None, None, :, None]
        shaped = jnp.where(allowed, shaped, neg_fill)
        block_top = jnp.max(shaped, axis=(4, 5)).reshape(tok_all, kv_heads, group)
        new_top = jnp.maximum(top, block_top)
        lifted = new_top.reshape(q_blocks, QB, kv_heads, group, 1, 1)
        weights = jnp.where(allowed, jnp.exp(shaped - lifted), 0.0).reshape(
            tok_all, kv_heads, group, block
        )
        factor = jnp.exp(top - new_top)
        total = total * factor + jnp.sum(weights, axis=-1)
        summed = summed * factor[..., None] + jnp.einsum(
            "tgjc,cgd->tgjd",
            weights.astype(jnp.bfloat16),
            values,
            preferred_element_type=jnp.float32,
        )
        return (new_top, total, summed)

    start_top = jnp.full((tok_all, kv_heads, group), neg_fill, jnp.float32)
    start_total = jnp.zeros((tok_all, kv_heads, group), jnp.float32)
    start_sum = jnp.zeros((tok_all, kv_heads, group, head_dim), jnp.float32)
    top, total, summed = lax.fori_loop(
        0, ctx_local // block, cache_step, (start_top, start_total, start_sum)
    )
    top = top.reshape(tok_all, all_heads)
    total = total.reshape(tok_all, all_heads)
    summed = summed.reshape(tok_all, all_heads, head_dim)
    got_sum, got_top, got_total = (
        lax.all_to_all(summed[None], "seq", split_axis=2, concat_axis=0, tiled=True),
        lax.all_to_all(top[None], "seq", split_axis=2, concat_axis=0, tiled=True),
        lax.all_to_all(total[None], "seq", split_axis=2, concat_axis=0, tiled=True),
    )
    cache_top = jnp.max(got_top, axis=0)
    factor = jnp.exp(got_top - cache_top[None])
    cache_total = jnp.sum(got_total * factor, axis=0)
    cache_sum = jnp.sum(got_sum * factor[..., None], axis=0)
    kv_index = (rank * own_heads + jnp.arange(own_heads, dtype=jnp.int32)) // group
    own_keys = jnp.take(key_rot, kv_index, axis=1)
    own_values = jnp.take(value_heads, kv_index, axis=1)
    own_q = own_query.reshape(tok_all, own_heads, head_dim)
    self_scores = (
        jnp.einsum("thd,shd->ths", own_q, own_keys, preferred_element_type=jnp.float32) * scale
    )
    row_ids = jnp.arange(tok_all, dtype=jnp.int32)
    causal = (row_ids[None, :] <= row_ids[:, None])[:, None, :]
    self_scores = jnp.where(causal, self_scores, neg_fill)
    top_all = jnp.maximum(cache_top, jnp.max(self_scores, axis=-1))
    cache_factor = jnp.exp(cache_top - top_all)
    self_weights = jnp.where(causal, jnp.exp(self_scores - top_all[..., None]), 0.0)
    total_all = cache_total * cache_factor + jnp.sum(self_weights, axis=-1)
    sum_all = cache_sum * cache_factor[..., None] + jnp.einsum(
        "ths,shd->thd",
        self_weights.astype(jnp.bfloat16),
        own_values,
        preferred_element_type=jnp.float32,
    )
    attention = (sum_all / total_all[..., None]).reshape(tok_all, query_cols).astype(jnp.bfloat16)
    projected = lax.psum_scatter(
        jnp.dot(attention, w_out[0], preferred_element_type=jnp.float32).astype(jnp.bfloat16),
        "seq",
        scatter_dimension=0,
        tiled=True,
    ).astype(jnp.float32)
    layer_out = (resid + projected).astype(jnp.bfloat16)
    handed = passed_along(layer_out, "section", 1)
    return handed[None]


MIB = 1 << 20
log2e = 1.4426950408889634
IN_VMEM = pl.BlockSpec(memory_space=pltpu.VMEM)
IN_SMEM = pl.BlockSpec(memory_space=pltpu.SMEM)
SAME_CORE = (2, 4, 6)
EVEN = (0, 2, 4, 6)
ODD = (1, 3, 5, 7)


def swapped(block, bits):
    n = lax.axis_size("seq")
    return lax.ppermute(block, "seq", [(i, i ^ bits) for i in range(n)])


def onward(block, bits):
    sections, n = lax.axis_size("section"), lax.axis_size("seq")
    route = [
        (s * n + i, (s + 1) % sections * n + (i ^ bits)) for s in range(sections) for i in range(n)
    ]
    return lax.ppermute(block, ("section", "seq"), route)


def call(kernel, name, out_shape, in_specs, flops=0, nbytes=0, scratch=(), vmem=6, **grid):
    out_specs = grid.pop("out_specs", jax.tree.map(lambda _: IN_VMEM, out_shape))
    return pl.pallas_call(
        kernel,
        out_shape=out_shape,
        in_specs=in_specs,
        out_specs=out_specs,
        scratch_shapes=list(scratch),
        name=name,
        cost_estimate=pl.CostEstimate(flops=flops, bytes_accessed=nbytes, transcendentals=0),
        compiler_params=pltpu.CompilerParams(vmem_limit_bytes=vmem * MIB),
        **grid,
    )


def held(array):
    return pltpu.with_memory_space_constraint(array, pltpu.VMEM)


def join_kernel(count, *refs):
    for i in range(count):
        refs[-1][i] = refs[i][...]


def joined_after(blocks, done, name):
    count = len(blocks)
    return call(
        lambda *refs: join_kernel(count, *refs),
        name,
        jax.ShapeDtypeStruct((count, *blocks[0].shape), blocks[0].dtype),
        [IN_VMEM] * count + [pl.BlockSpec(memory_space=pl.ANY)] * len(done),
        nbytes=MIB,
        vmem=2,
    )(*blocks, *done)


def rotated(heads, cosine, sine):
    half = heads.shape[1] // 2
    return heads * cosine + pltpu.roll(heads, half, 1) * sine


def query_kernel(rank, *refs):
    same_core, other_core, gain, cosine, sine, weights, query, normed, rows = refs
    width = rows.shape[1]
    count = same_core.shape[1]
    blocks = [part.at[i] for i in range(4) for part in (same_core, other_core)]
    step = 1024
    for bits in range(8):
        at = pl.multiple_of((rank[0] ^ bits) * count, count)
        rows[pl.ds(at, count), :] = blocks[bits][...].astype(jnp.float32)
    squares = jnp.zeros((rows.shape[0], 128), jnp.float32)
    for c in range(0, width, 128):
        part = rows[:, c : c + 128]
        squares = squares + part * part
    mean_square = jnp.sum(squares, axis=-1, keepdims=True) / width
    factor = lax.rsqrt(mean_square + norm_eps)
    for c in range(0, width, step):
        normed[:, c : c + step] = (
            rows[:, c : c + step] * factor * gain[:, c : c + step].astype(jnp.float32)
        ).astype(jnp.bfloat16)
    dim = cosine.shape[1]
    for c in range(0, weights.shape[1], 2 * dim):
        raw = jnp.dot(
            normed[...], weights[:, c : c + 2 * dim], preferred_element_type=jnp.float32
        )
        for d in range(0, 2 * dim, dim):
            query[:, c + d : c + d + dim] = rotated(
                raw[:, d : d + dim], cosine[...], sine[...]
            ).astype(jnp.bfloat16)


def query_rows(query, q_block, heads, dim):
    rows = slice(q_block * QB, (q_block + 1) * QB)
    return jnp.concatenate([query[rows, j * dim : (j + 1) * dim] for j in range(heads)], axis=0)


def matmul_nt(a, b):
    return lax.dot_general(a, b, (((1,), (1,)), ((), ())), preferred_element_type=jnp.float32)


def by_head_kernel(rank, keys, values, keys_out, values_out, done, keys_in, values_in, sems):
    blocks = sems.shape[1]
    block = keys.shape[0] // blocks

    def copies(i):
        at = pl.ds(pl.multiple_of(i * block, block), block)
        return [
            pltpu.make_async_copy(source.at[at], target.at[at], sems.at[which, i])
            for which, (source, target) in enumerate([(keys, keys_in), (values, values_in)])
        ]

    @pl.loop(0, blocks)
    def _(i):
        for copy in copies(i):
            copy.start()

    done[...] = jnp.zeros_like(done)

    @pl.loop(0, blocks)
    def _(i):
        at = pl.ds(pl.multiple_of(i * block, block), block)
        for copy in copies(i):
            copy.wait()
        keys_out[:, at, :] = jnp.swapaxes(keys_in[at], 0, 1)
        turned = jnp.swapaxes(values_in[at], 0, 1)
        for g in range(turned.shape[0]):
            values_out[g, :, at] = turned[g].T


def cache_by_head(rank, keys, values):
    ctx, heads, dim = keys.shape
    blocks = 8
    in_hbm = pl.BlockSpec(memory_space=pltpu.HBM)
    return call(
        by_head_kernel,
        "cache_by_head",
        [
            jax.ShapeDtypeStruct((heads, ctx, dim), jnp.bfloat16),
            jax.ShapeDtypeStruct((heads, dim, ctx), jnp.bfloat16),
            jax.ShapeDtypeStruct((8, 128), jnp.float32),
        ],
        [IN_SMEM, in_hbm, in_hbm],
        flops=10**10,
        nbytes=ctx * heads * dim * 2,
        scratch=[
            pltpu.VMEM(keys.shape, jnp.bfloat16),
            pltpu.VMEM(values.shape, jnp.bfloat16),
            pltpu.SemaphoreType.DMA((2, blocks)),
        ],
        vmem=14,
    )(
        rank,
        pltpu.with_memory_space_constraint(keys, pltpu.HBM),
        pltpu.with_memory_space_constraint(values, pltpu.HBM),
    )


def new_kernel(
    scale,
    query,
    normed,
    w_key,
    w_value,
    cosine,
    sine,
    summed,
    stats,
):
    tok, dim = cosine.shape
    heads = query.shape[1] // dim
    raw = jnp.dot(normed[...], w_key[...], preferred_element_type=jnp.float32)
    raw = raw.astype(jnp.bfloat16).astype(jnp.float32)
    keys = rotated(raw, cosine[...], sine[...]).astype(jnp.bfloat16)
    values = jnp.dot(normed[...], w_value[...], preferred_element_type=jnp.float32)
    values = values.astype(jnp.bfloat16).astype(jnp.float32).T.astype(jnp.bfloat16)
    cols = heads * QB
    for q_block in range(tok // QB):
        scores = matmul_nt(keys, query_rows(query, q_block, heads, dim)) * scale
        u = lax.broadcasted_iota(jnp.int32, (tok, cols), 0)
        t = lax.broadcasted_iota(jnp.int32, (tok, cols), 1) % QB + q_block * QB
        allowed = u <= t
        scores = jnp.where(allowed, scores, neg_fill)
        top = jnp.max(scores, axis=0, keepdims=True)
        weights = jnp.where(allowed, jnp.exp2(scores - top), 0.0)
        at = slice(q_block * cols, (q_block + 1) * cols)
        stats[0:1, at] = top
        stats[1:2, at] = jnp.sum(weights, axis=0, keepdims=True)
        summed[:, at] = jnp.dot(
            values, weights.astype(jnp.bfloat16), preferred_element_type=jnp.float32
        )


def split_rows(level, rows):
    high = level.astype(jnp.bfloat16).astype(jnp.float32)
    rest = level - high
    middle = rest.astype(jnp.bfloat16).astype(jnp.float32)
    low = rest - middle
    row = lax.broadcasted_iota(jnp.int32, (rows, level.shape[1]), 0)
    return jnp.where(row == 0, high, jnp.where(row == 1, middle, jnp.where(row == 2, low, 0.0)))


def level_of(tail):
    tail = tail.astype(jnp.float32)
    return tail[0:1] + tail[1:2] + tail[2:3]


def cache_kernel(scale, order, rank, mask, *refs):
    n = len(order)
    given = 1 if len(refs[0].shape) == 3 else n
    queries, (keys, values), outs = refs[:given], refs[given : given + 2], refs[given + 2 : -5]
    if given < n:
        queries = [queries[0].at[i] for i in range(n)]
    q_rows, summed, visible, scores, levels = refs[-5:]
    dim = keys.shape[2]
    heads = queries[0].shape[1] // dim
    cols = heads * QB
    groups = [rank[0] ^ bits for bits in order]
    own = [bits for bits in order if bits in EVEN]
    blocks = mask.shape[0]
    place = jnp.int32(0)
    ends, singles = [], []
    for q_block in range(blocks):
        for b in range(mask.shape[1]):
            visible[place] = b
            place = place + (mask[q_block, b] > 0).astype(jnp.int32)
        visible[place] = 0
        odd = place % 2
        place = place + odd
        ends.append(place // 2)
        singles.append(jnp.where(odd == 1, place // 2 - 1, -1))
        for i in range(n):
            q_rows[q_block, i] = query_rows(queries[i], q_block, heads, dim)
            summed[q_block, i] = jnp.zeros((dim, cols), jnp.float32)
            levels[q_block, i, 0:1] = jnp.full((1, cols), neg_fill, jnp.float32)
            levels[q_block, i, 1:2] = jnp.zeros((1, cols), jnp.float32)
    for e in range(2):
        visible[place + e] = 0

    def q_block_of(pair):
        return sum((pair >= end).astype(jnp.int32) for end in ends[:-1])

    def places(pair):
        return [pl.multiple_of(visible[2 * pair + e] * KB, KB) for e in range(2)]

    def score(pair):
        at = places(pair)
        q_block = q_block_of(pair)
        single = functools.reduce(jnp.logical_or, [pair == one for one in singles])
        hidden = jnp.where(single, jnp.float32(neg_fill), jnp.float32(0.0))
        products = [
            matmul_nt(
                jnp.concatenate([keys[g, pl.ds(a, KB), :] for a in at], axis=0),
                q_rows[q_block, i],
            )
            for i, g in enumerate(groups)
        ]
        tops = []
        for i in range(n):
            first = products[i][:KB] * scale
            second = products[i][KB:] * scale + hidden
            scores[i, :KB] = first
            scores[i, KB:] = second
            tops.append(jnp.max(jnp.maximum(first, second), axis=0, keepdims=True))
        return tops

    def step(pair, tops):
        q_block = q_block_of(pair)
        scaled = []
        for i in range(n):
            top, total = levels[q_block, i, 0:1], levels[q_block, i, 1:2]
            new_top = jnp.maximum(top, tops[i])
            weights = jnp.exp2(scores[i] - new_top)
            factor = jnp.exp2(top - new_top)
            levels[q_block, i, 0:1] = new_top
            levels[q_block, i, 1:2] = total * factor + jnp.sum(weights, axis=0, keepdims=True)
            scaled.append((factor, weights.astype(jnp.bfloat16)))
        at = places(pair)
        products = [
            jnp.dot(
                jnp.concatenate([values[g, :, pl.ds(a, KB)] for a in at], axis=1),
                scaled[i][1],
                preferred_element_type=jnp.float32,
            )
            for i, g in enumerate(groups)
        ]
        tops = score(pair + 1)
        for i in range(n):
            summed[q_block, i] = summed[q_block, i] * scaled[i][0] + products[i]
        return tuple(tops)

    lax.fori_loop(0, ends[-1], step, tuple(score(jnp.int32(0))))
    for q_block in range(blocks):
        at = slice(q_block * cols, (q_block + 1) * cols)
        for i, bits in enumerate(order):
            top, total = levels[q_block, i, 0:1], levels[q_block, i, 1:2]
            seen = total > 0.0
            safe = jnp.where(seen, total, 1.0)
            level = jnp.where(seen, top + jnp.log2(safe), neg_fill)
            if bits in EVEN:
                out, place = outs[0], own.index(bits)
            else:
                out, place = outs[-1], i - len(own)
            out[place, 0:dim, at] = (summed[q_block, i] * (1.0 / safe)).astype(out.dtype)
            out[place, dim:, at] = split_rows(level, out.shape[1] - dim).astype(out.dtype)


def cache_part(scale, order, rank, mask, queries, keys, values, name):
    heads, ctx, dim = keys.shape
    cols = (queries[0].shape[-1] // dim) * QB
    n = len(order)
    own = len([bits for bits in order if bits in EVEN])
    outs = []
    if own:
        outs.append(jax.ShapeDtypeStruct((own, dim + 8, mask.shape[0] * cols), jnp.float32))
    if n > own:
        outs.append(jax.ShapeDtypeStruct((n - own, dim + 16, mask.shape[0] * cols), jnp.bfloat16))
    return call(
        lambda *refs: cache_kernel(scale, order, *refs),
        name,
        outs,
        [IN_SMEM, IN_SMEM] + [IN_VMEM] * (len(queries) + 2),
        flops=(2 if own else 10) * n * queries[0].shape[-2] * heads * ctx * dim,
        nbytes=n * MIB,
        scratch=[
            pltpu.VMEM((mask.shape[0], n, cols, dim), jnp.bfloat16),
            pltpu.VMEM((mask.shape[0], n, dim, cols), jnp.float32),
            pltpu.SMEM((mask.size + 4,), jnp.int32),
            pltpu.VMEM((n, 2 * KB, cols), jnp.float32),
            pltpu.VMEM((mask.shape[0], n, 8, cols), jnp.float32),
        ],
    )(rank, mask, *queries, held(keys), held(values))


def merge_kernel(own_first, own_rest, got_first, got_rest, kept, *sent):
    dim = own_first.shape[1] - 8
    for i in range(4):
        own = own_first.at[0] if i == 0 else own_rest.at[i - 1]
        got = got_first.at[0] if i == 0 else got_rest.at[i - 1]
        mine, other = level_of(own[dim:, :]), level_of(got[dim:, :])
        top = jnp.maximum(mine, other)
        mine, other = jnp.exp2(mine - top), jnp.exp2(other - top)
        total = mine + other
        level = top + jnp.log2(total)
        mine, other = mine / total, other / total
        joined = own[:dim, :] * mine + got[:dim, :].astype(jnp.float32) * other
        target = kept if i == 0 else sent[i - 1]
        target[:dim, :] = joined.astype(target.dtype)
        target[dim:, :] = split_rows(level, target.shape[0] - dim).astype(target.dtype)


def output_kernel(
    rank,
    kept,
    got_a,
    got_b,
    got_c,
    summed,
    stats,
    weights,
    own,
    sent_near,
    sent_far,
    rows,
    sorted_rows,
):
    dim = summed.shape[0]
    levels = [level_of(part[dim:, :]) for part in (kept, got_a, got_b, got_c)]
    top = stats[0:1, :]
    for level in levels:
        top = jnp.maximum(top, level)
    factor = jnp.exp2(stats[0:1, :] - top)
    total = stats[1:2, :] * factor
    joined = summed[...] * factor
    for part, level in zip((kept, got_a, got_b, got_c), levels):
        factor = jnp.exp2(level - top)
        total = total + factor
        joined = joined + part[:dim, :].astype(jnp.float32) * factor
    joined = joined * (1.0 / total)
    heads = rows.shape[1] // dim
    cols = heads * QB
    for q_block in range(rows.shape[0] // QB):
        turned = joined[:, q_block * cols : (q_block + 1) * cols].T
        for j in range(heads):
            rows[q_block * QB : (q_block + 1) * QB, j * dim : (j + 1) * dim] = turned[
                j * QB : (j + 1) * QB, :
            ]
    count = rows.shape[0] // 8
    for pair in range(4):
        chunk = [
            rows[pl.ds(pl.multiple_of((rank[0] ^ bits) * count, count), count), :]
            for bits in (EVEN + ODD)[2 * pair : 2 * pair + 2]
        ]
        sorted_rows[2 * count * pair : 2 * count * (pair + 1), :] = jnp.concatenate(
            chunk, axis=0
        ).astype(jnp.bfloat16)
    half = rows.shape[0] // 2
    step = 512
    for c in range(0, weights.shape[1], step):
        product = jnp.dot(
            sorted_rows[...], weights[:, c : c + step], preferred_element_type=jnp.float32
        )
        own[:, c : c + step] = product[:half]
        sent = product[half:].astype(jnp.bfloat16)
        sent_near[:, c : c + step] = sent[: half // 2]
        sent_far[:, c : c + step] = sent[half // 2 :]


def pair_kernel(first, own, got, *outs, resid=None):
    count = outs[0].shape[0]
    other = got[...].astype(jnp.float32)
    for i, out in enumerate(outs):
        block = own[(first + i) * count : (first + i + 1) * count]
        block = block + other[i * count : (i + 1) * count]
        if resid is not None and i == 0:
            block = resid[...].astype(jnp.float32) + block
        out[...] = block.astype(out.dtype)


def add_kernel(block, across, out):
    out[...] = (block[...] + across[...].astype(jnp.float32)).astype(out.dtype)


def on_device_owned(
    tokens,
    norm_gain,
    w_query,
    key_projection,
    value_projection,
    w_out,
    key_cache,
    cached_value_rows,
    cache_mask,
    span_offset,
):
    n_seq = lax.axis_size("seq")
    rank = lax.axis_index("seq").astype(jnp.int32)[None]
    dim = key_cache.shape[3]
    count = tokens.shape[1]
    width = tokens.shape[2]
    tok = count * n_seq
    own_cols = w_query.shape[2]
    scale = dim ** (-0.5) * log2e
    mask = cache_mask[0]

    with jax.named_scope("cache_layout"):
        keys, values, layout_done = cache_by_head(rank, key_cache[0], cached_value_rows[0])
    with jax.named_scope("gather_tokens"):
        blocks = {0: tokens[0]}
        for bits in SAME_CORE:
            blocks[bits] = swapped(blocks[0], bits)
        same_core = joined_after([blocks[bits] for bits in EVEN], [layout_done], "join_tokens")
        other_core = swapped(same_core, 1)

    with jax.named_scope("tables"):
        positions = span_offset[0].astype(jnp.float32) + jnp.arange(tok, dtype=jnp.int32).astype(
            jnp.float32
        )
        freqs = rope_base ** (-2.0 * jnp.arange(dim // 2, dtype=jnp.float32) / dim)
        angles = positions[:, None] * freqs[None, :]
        cosine, sine = jnp.cos(angles), jnp.sin(angles)
        cosine = jnp.concatenate([cosine, cosine], axis=1)
        sine = jnp.concatenate([-sine, sine], axis=1)

    with jax.named_scope("queries"):
        query, normed = call(
            query_kernel,
            "queries",
            [
                jax.ShapeDtypeStruct((tok, own_cols), jnp.bfloat16),
                jax.ShapeDtypeStruct((tok, width), jnp.bfloat16),
            ],
            [IN_SMEM] + [IN_VMEM] * 6,
            flops=8 * tok * width * own_cols // 2,
            nbytes=16 * MIB,
            scratch=[pltpu.VMEM((tok, width), jnp.float32)],
        )(
            rank,
            same_core,
            other_core,
            norm_gain,
            cosine,
            sine,
            held(w_query[0]),
        )

    with jax.named_scope("gather_queries"):
        queries = {0: query}
        for bits in ODD:
            queries[bits] = swapped(query, bits)
    with jax.named_scope("new_tokens"):
        summed, stats = call(
            lambda *refs: new_kernel(scale, *refs),
            "new_tokens",
            [
                jax.ShapeDtypeStruct((dim, tok * own_cols // dim), jnp.float32),
                jax.ShapeDtypeStruct((8, tok * own_cols // dim), jnp.float32),
            ],
            [IN_VMEM] * 6,
            flops=16 * tok * width * dim,
            nbytes=5 * MIB,
        )(
            query,
            normed,
            held(key_projection[0]),
            held(value_projection[0]),
            cosine,
            sine,
        )

    with jax.named_scope("cache_near"):
        near_own, near_sent = cache_part(
            scale, (0, 1), rank, mask, [queries[0], queries[1]], keys, values, "cache_near"
        )
        near_got = swapped(near_sent, 1)
    with jax.named_scope("gather_queries"):
        far_odd = joined_after([queries[bits] for bits in ODD[1:]], [near_own], "join_queries")
        far_even = swapped(far_odd, 1)
    with jax.named_scope("cache_odd"):
        (odd,) = cache_part(scale, ODD[1:], rank, mask, [far_odd], keys, values, "cache_odd")
        odd_got = swapped(odd, 1)
    with jax.named_scope("cache_even"):
        (even,) = cache_part(scale, EVEN[1:], rank, mask, [far_even], keys, values, "cache_even")
    with jax.named_scope("merge_cores"):
        cols = even.shape[2]
        kept, *sent = call(
            merge_kernel,
            "merge_cores",
            [jax.ShapeDtypeStruct((dim + 8, cols), jnp.float32)]
            + [jax.ShapeDtypeStruct((dim + 16, cols), jnp.bfloat16)] * 3,
            [IN_VMEM] * 4,
            nbytes=2 * MIB,
        )(near_own, even, near_got, odd_got)
    with jax.named_scope("exchange_parts"):
        parts = [swapped(block, bits) for block, bits in zip(sent, SAME_CORE)]
    with jax.named_scope("project"):
        own, near, far = call(
            output_kernel,
            "project",
            [
                jax.ShapeDtypeStruct((tok // 2, width), jnp.float32),
                jax.ShapeDtypeStruct((tok // 4, width), jnp.bfloat16),
                jax.ShapeDtypeStruct((tok // 4, width), jnp.bfloat16),
            ],
            [IN_SMEM] + [IN_VMEM] * 7,
            flops=8 * tok * width * own_cols // 2,
            nbytes=18 * MIB,
            scratch=[
                pltpu.VMEM((tok, own_cols), jnp.float32),
                pltpu.VMEM((tok, own_cols), jnp.bfloat16),
            ],
        )(rank, kept, *parts, summed, stats, held(w_out[0]))
    with jax.named_scope("reduce_cores"):
        row = jax.ShapeDtypeStruct((count, width), jnp.bfloat16)
        row_f32 = jax.ShapeDtypeStruct((count, width), jnp.float32)
        at_y, to_x = call(
            lambda *refs: pair_kernel(2, *refs),
            "reduce_far",
            [row_f32, row],
            [IN_VMEM] * 2,
            nbytes=MIB,
        )(own, swapped(far, 1))
        at_own, at_x = call(
            lambda own, got, resid, *outs: pair_kernel(0, own, got, *outs, resid=resid),
            "reduce_near",
            [row, row],
            [IN_VMEM] * 3,
            nbytes=MIB,
        )(own, swapped(near, 1), tokens[0])
    with jax.named_scope("reduce_on_next_section"):
        across = swapped(to_x, EVEN[1])
        from_own, from_x = onward(at_own, EVEN[0]), onward(at_x, EVEN[1])
        at_y = call(add_kernel, "add_across", row, [IN_VMEM] * 2)(at_y, across)
        total = from_own.astype(jnp.float32) + from_x.astype(jnp.float32)
        total = total + onward(at_y, EVEN[2]).astype(jnp.float32)
        handed = total.astype(jnp.bfloat16)
    return handed[None]


def on_device(*arrays):
    tokens, w_query, key_projection, key_cache = arrays[0], arrays[2], arrays[3], arrays[6]
    head_dim = key_cache.shape[3]
    kv_heads = key_cache.shape[2]
    n_seq = lax.axis_size("seq")
    tok_all = tokens.shape[1] * n_seq
    if (
        n_seq == kv_heads == 8
        and key_projection.shape[2] == head_dim == 128
        and tokens.shape[1] == 8
        and tok_all == 2 * QB
    ):
        return on_device_owned(*arrays)
    return on_device_any(*arrays)


def solution(mesh):
    placed = (
        P("section", "seq", None),
        P("section", None),
        P("section", None, "seq"),
        P("section", None, "seq"),
        P("section", None, "seq"),
        P("section", "seq", None),
        P("section", "seq", None, None),
        P("section", "seq", None, None),
        P("section", None, "seq"),
        P("section"),
    )
    return jax.shard_map(
        on_device, mesh=mesh, in_specs=placed, out_specs=P("section", "seq", None), check_vma=False
    )
```
